1024 devices in a mesh: dom: 128 (over y, z), sub: 8 (over x, core).
Axes of the slice: x: 4, y: 8, z: 16, core: 2. Of those that a mesh axis runs over, the one named last changes fastest.
Arguments:
- a_tiles: bfloat16 [8192, 8, 128, 128], P(('dom', 'sub')), may hold values from -0.5 to 0.5
- col_tiles: int32 [8192, 8], P(('dom', 'sub')), may hold values from 0 to 8191, as said below
- counts: int32 [8192], P(('dom', 'sub')), may hold values from 1 to 8, as said below
- aggregate: int32 [8192], P(('dom', 'sub')), may hold values from 0 to 511, as said below
- p_tiles: bfloat16 [8192, 128, 128], P(('dom', 'sub')), may hold values from -0.25 to 0.25
Outputs:
- coarse: float32 [65536, 1536], P(('dom', 'sub'))
The draws below stay inside these ranges and needn't reach their ends.
Inputs may be any that keep to these rules, and one draw needn't show every extreme that they name: `col_tiles`: slot 0 of each row names the row itself. A column of a row of device (g, s) lies on device (g, s), on device (g - 1 mod 128, s) among its last 2 rows, or on device (g + 1 mod 128, s) among its first 2 rows. `counts`: the first row of every device has 8 live slots. `aggregate`: rows of group g name coarse tiles g * 4 to g * 4 + 3.
All inputs are finite; a program needn't handle non-finite values.
Results may differ from the reference program's by a relative error of at most 0.012.
Values may be sent and summed in bfloat16 or wider, within the bound.
No kernel may reach another device: no remote copies, remote signals or barrier semaphores. Data moves between devices by JAX's collectives and lax.ppermute only.
A program may use at most 32 MiB of HBM per device.

```python
import jax
import jax.numpy as jnp
from jax import lax

B = 128
K = 8
CG = 4
R = 8
HALO = 2
NF = 8192
N_DOM = 128
N_SUB = 8


def draw_col_tiles(key, part):
    key = jax.random.fold_in(key, 11)
    key_side, key_own, key_edge = jax.random.split(key, 3)
    tile_ids = jnp.arange(NF, dtype=jnp.int32)
    device_ids = tile_ids // R
    row_group = device_ids // N_SUB
    row_member = device_ids % N_SUB
    side_pick = jax.random.randint(key_side, (NF, K), 0, 4)
    offset = jnp.where(side_pick == 0, 0, jnp.where(side_pick == 3, 2, 1))
    own_local = jax.random.randint(key_own, (NF, K), 0, R)
    edge_local = jax.random.randint(key_edge, (NF, K), 0, HALO)
    local_idx = jnp.where(offset == 0, R - HALO + edge_local, jnp.where(offset == 2, edge_local, own_local))
    near_group = (row_group[:, None] + offset - 1) % N_DOM
    columns = (near_group * N_SUB + row_member[:, None]) * R + local_idx
    slot_ids = jnp.arange(K, dtype=jnp.int32)[None, :]
    columns = jnp.where(slot_ids == 0, tile_ids[:, None], columns)
    return columns.astype(jnp.int32)


def draw_counts(key, part):
    key = jax.random.fold_in(key, 23)
    tile_ids = jnp.arange(NF, dtype=jnp.int32)
    drawn = jax.random.randint(key, (NF,), 1, K + 1)
    return jnp.where(tile_ids % R == 0, K, drawn).astype(jnp.int32)


def draw_aggregate(key, part):
    key = jax.random.fold_in(key, 37)
    tile_ids = jnp.arange(NF, dtype=jnp.int32)
    row_group = tile_ids // (R * N_SUB)
    drawn = jax.random.randint(key, (NF,), 0, CG)
    return (row_group * CG + drawn).astype(jnp.int32)


def block_scale(stream_key, dims, shards, smallest, largest):
    gain = 1.0
    for axis_at, shards_of in shards:
        heights = jax.random.uniform(jax.random.fold_in(jax.random.fold_in(stream_key, 6), axis_at), (shards_of,), jnp.float32, smallest / len(shards), largest / len(shards))
        gain = gain * jnp.repeat(jnp.exp(heights), dims[axis_at] // shards_of).reshape((-1,) + (1,) * (len(dims) - 1 - axis_at))
    return gain


def gaussian(stream_key, dims, deviation, limit, shards=(), held_as=jnp.bfloat16):
    values = jax.random.normal(stream_key, dims, jnp.float32) * deviation
    if len(shards) > 0:
        values = block_scale(stream_key, dims, shards, -0.22, 0.18) * values
    return jnp.clip(values, min=-limit, max=limit).astype(held_as)


def setup_inputs(seed: int = 0) -> dict:
    streams_of = jax.random.split(jax.random.key(seed), 6)
    a_tiles = gaussian(streams_of[0], (NF, K, B, B), B ** -0.5, 0.5, ((0, 1024),))
    col_tiles = draw_col_tiles(jax.random.fold_in(streams_of[5], 71), 0)
    counts = draw_counts(jax.random.fold_in(streams_of[5], 71), 0)
    aggregate = draw_aggregate(jax.random.fold_in(streams_of[5], 71), 0)
    p_tiles = gaussian(streams_of[4], (NF, B, B), (4 * B) ** -0.5, 0.25, ((0, 1024),))
    return {"a_tiles": a_tiles, "col_tiles": col_tiles, "counts": counts, "aggregate": aggregate, "p_tiles": p_tiles}


def device_slab(a_part, col_part, count_part, agg_part, p_part, p_all, agg_all, my_group):
    slots = 3 * CG * CG
    near_p = p_all[col_part].astype(jnp.float32)
    prod = jnp.einsum("rkab,rkbc->rkac", a_part.astype(jnp.float32), near_p).astype(jnp.bfloat16)
    term = jnp.einsum("rba,rkbc->rkac", p_part.astype(jnp.float32), prod.astype(jnp.float32))
    col_group = col_part // (R * N_SUB)
    offset = (col_group - my_group + 1) % N_DOM
    coarse_col = offset * CG + agg_all[col_part] - col_group * CG
    coarse_row = agg_part - my_group * CG
    slot_ids = coarse_row[:, None] * (3 * CG) + coarse_col
    live = jnp.arange(K, dtype=jnp.int32)[None, :] < count_part[:, None]
    onehot = ((slot_ids[:, :, None] == jnp.arange(slots, dtype=jnp.int32)[None, None, :]) & live[:, :, None]).astype(jnp.float32)
    summed = jnp.einsum("rks,rkac->sac", onehot, term, precision=lax.Precision.HIGHEST)
    summed = summed.reshape(CG, 3 * CG, B, B).transpose(0, 2, 1, 3).reshape(CG * B, 3 * CG * B)
    return summed.astype(jnp.bfloat16)


def reference(a_tiles, col_tiles, counts, aggregate, p_tiles):
    a_dev = a_tiles.reshape(N_DOM, N_SUB, R, K, B, B)
    col_dev = col_tiles.reshape(N_DOM, N_SUB, R, K)
    cnt_dev = counts.reshape(N_DOM, N_SUB, R)
    agg_dev = aggregate.reshape(N_DOM, N_SUB, R)
    p_dev = p_tiles.reshape(N_DOM, N_SUB, R, B, B)

    def one_group(inputs):
        my_group, a_grp, col_grp, cnt_grp, agg_grp, p_grp = inputs
        total = jnp.zeros((CG * B, 3 * CG * B), jnp.float32)
        for member in range(N_SUB):
            piece = device_slab(a_grp[member], col_grp[member], cnt_grp[member], agg_grp[member], p_grp[member], p_tiles, aggregate, my_group)
            total = total + piece.astype(jnp.float32)
        return total

    group_ids = jnp.arange(N_DOM, dtype=jnp.int32)
    result = lax.map(one_group, (group_ids, a_dev, col_dev, cnt_dev, agg_dev, p_dev))
    return result.reshape(N_DOM * CG * B, 3 * CG * B)
```

```python
import functools

import jax
import jax.numpy as jnp
from jax import lax
from jax.experimental import pallas as pl
from jax.experimental.pallas import tpu as pltpu
from jax.sharding import PartitionSpec as P

CG = 4
HALO = 2
MARK = 16


def front_kernel(groups, members, col_ref, count_ref, agg_ref, a_hbm, p_ref, g_ref, own_ref, a_ref, acc_ref, gown_ref, place_ref, sems):
    rows, slots, tile = a_hbm.shape[0], a_hbm.shape[1], a_hbm.shape[2]
    columns = rows + 2 * HALO
    half = tile // 2
    copies = [pltpu.make_async_copy(a_hbm.at[t], a_ref.at[t], sems.at[t]) for t in range(rows)]
    for copy in copies:
        copy.start()
    acc_ref[...] = jnp.zeros_like(acc_ref)
    device = col_ref[0, 0] // rows
    my_group = device // members
    core = device % 2
    for r in range(rows):
        coarse = agg_ref[r] - my_group * CG
        for j in range(CG):
            place_ref[pl.ds(r * tile, tile), pl.ds(j * tile, tile)] = jnp.where(coarse == j, p_ref[r], jnp.zeros_like(p_ref[r]))
    for t in range(rows):
        coarse = agg_ref[t] - my_group * CG
        p_t = p_ref[t].T
        copies[t].wait()
        for pair in range(slots // 2):
            both = jnp.concatenate([a_ref[t, 2 * pair], a_ref[t, 2 * pair + 1]], axis=1)
            terms = jnp.dot(p_t, both, preferred_element_type=jnp.float32)
            for side in range(2):
                k = 2 * pair + side
                column = col_ref[t, k]
                side_of = column // (rows * members) - my_group + 1 + groups
                side_of = lax.rem(side_of, groups)
                near = lax.rem(column, rows) + rows * side_of - (rows - HALO)
                at = jnp.where(k < count_ref[t], coarse * columns + near, CG * columns)
                at = jnp.clip(at, 0, CG * columns)
                acc_ref[at] += terms[:, side * tile : (side + 1) * tile]
    for i in range(CG):
        for part in range(2):
            first = pl.multiple_of((core if part == 1 else 1 - core) * half, half)
            to = pl.ds((part * CG + i) * half, half)
            for c in range(columns):
                block = acc_ref[i * columns + c, pl.ds(first, half), :].astype(jnp.bfloat16)
                if c < HALO:
                    g_ref[to, pl.ds(c * tile, tile)] = block
                elif c >= HALO + rows:
                    g_ref[to, pl.ds((c - rows) * tile, tile)] = block
                else:
                    gown_ref[to, pl.ds((c - HALO) * tile, tile)] = block
    own_ref[...] = jnp.dot(gown_ref[...], place_ref[...], preferred_element_type=jnp.float32).astype(jnp.bfloat16)


def back_kernel(g_ref, own_ref, before_ref, ahead_ref, out_ref, send_ref, place_ref):
    tile = before_ref.shape[1]
    rows = out_ref.shape[0]
    for side, halo_ref in enumerate((before_ref, ahead_ref)):
        for r in range(HALO):
            block = halo_ref[pl.ds(r * tile, tile), :]
            mark = halo_ref[pl.ds(HALO * tile + r * MARK, MARK), :].astype(jnp.float32)[0:1, :]
            for j in range(CG):
                chosen = jnp.where(mark == float(j), 1.0, 0.0).astype(jnp.bfloat16)
                place_ref[side, pl.ds(r * tile, tile), pl.ds(j * tile, tile)] = block * chosen
    width = CG * tile
    for side in range(2):
        depth = HALO * tile
        result = jnp.dot(g_ref[:, pl.ds(side * depth, depth)], place_ref[side], preferred_element_type=jnp.float32).astype(jnp.bfloat16)
        at = pl.ds(2 * side * width, width)
        send_ref[:, at] = result[:rows]
        out_ref[:, at] = result[rows:]
    send_ref[:, pl.ds(width, width)] = own_ref[pl.ds(0, rows), :]
    out_ref[:, pl.ds(width, width)] = own_ref[pl.ds(rows, rows), :]


def local(groups, members, a_tiles, col_tiles, counts, aggregate, p_tiles):
    rows, slots, tile = a_tiles.shape[0], a_tiles.shape[1], a_tiles.shape[2]
    columns = rows + 2 * HALO
    my_group = lax.axis_index("dom")
    coarse = (aggregate - my_group * CG).astype(jnp.bfloat16)

    def halo(first, step):
        marks = jnp.broadcast_to(coarse[first : first + HALO, None, None], (HALO, MARK, tile)).reshape(HALO * MARK, tile)
        block = jnp.concatenate([p_tiles[first : first + HALO].reshape(HALO * tile, tile), marks], axis=0)
        return lax.ppermute(block, "dom", [(i, (i + step) % groups) for i in range(groups)])

    before = halo(rows - HALO, 1)
    ahead = halo(0, -1)

    smem = pl.BlockSpec(memory_space=pltpu.SMEM)
    vmem = pl.BlockSpec(memory_space=pltpu.VMEM)
    g, own = pl.pallas_call(
        functools.partial(front_kernel, groups, members),
        out_shape=(
            jax.ShapeDtypeStruct((CG * tile, 2 * HALO * tile), jnp.bfloat16),
            jax.ShapeDtypeStruct((CG * tile, CG * tile), jnp.bfloat16),
        ),
        in_specs=[smem, smem, smem, pl.BlockSpec(memory_space=pl.ANY), vmem],
        out_specs=(vmem, vmem),
        scratch_shapes=[
            pltpu.VMEM(a_tiles.shape, jnp.bfloat16),
            pltpu.VMEM((CG * columns + 1, tile, tile), jnp.float32),
            pltpu.VMEM((CG * tile, rows * tile), jnp.bfloat16),
            pltpu.VMEM((rows * tile, CG * tile), jnp.bfloat16),
            pltpu.SemaphoreType.DMA((rows,)),
        ],
        compiler_params=pltpu.CompilerParams(vmem_limit_bytes=24 * 2**20),
        cost_estimate=pl.CostEstimate(flops=2 * 10**9, bytes_accessed=4 * 2**20, transcendentals=0),
        name="front",
    )(col_tiles, counts, aggregate, a_tiles, p_tiles)

    share = CG * tile // 2
    keep, send = pl.pallas_call(
        back_kernel,
        out_shape=(jax.ShapeDtypeStruct((share, 3 * CG * tile), jnp.bfloat16),) * 2,
        in_specs=[vmem] * 4,
        out_specs=(vmem, vmem),
        scratch_shapes=[pltpu.VMEM((2, HALO * tile, CG * tile), jnp.bfloat16)],
        compiler_params=pltpu.CompilerParams(vmem_limit_bytes=24 * 2**20),
        cost_estimate=pl.CostEstimate(flops=3 * 10**8, bytes_accessed=3 * 2**20, transcendentals=0),
        name="back",
    )(g, own, before, ahead)
    other = lax.ppermute(send, "sub", [(i, i ^ 1) for i in range(members)])
    chip = (keep.astype(jnp.float32) + other.astype(jnp.float32)).astype(jnp.bfloat16)
    cores = [list(range(core, members, 2)) for core in range(2)]
    parts = lax.all_to_all(chip.reshape(members // 2, -1, chip.shape[1]), "sub", 0, 0, axis_index_groups=cores)
    return parts.astype(jnp.float32).sum(axis=0)


def solution(mesh):
    in_specs = (
        P(("dom", "sub"), None, None, None),
        P(("dom", "sub"), None),
        P(("dom", "sub")),
        P(("dom", "sub")),
        P(("dom", "sub"), None, None),
    )
    out_specs = P(("dom", "sub"), None)
    body = functools.partial(local, mesh.shape["dom"], mesh.shape["sub"])
    return jax.shard_map(body, mesh=mesh, in_specs=in_specs, out_specs=out_specs, check_vma=False)
```

```python
import functools

import jax
import jax.numpy as jnp
from jax import lax
from jax.experimental import pallas as pl
from jax.experimental.pallas import tpu as pltpu
from jax.sharding import PartitionSpec as P

CG = 4
HALO = 2
MARK = 16
CORE = 64


def front_kernel(table_ref, a_hbm, p_ref, g_ref, own_ref, a_ref, acc_ref, gown_ref, place_ref, sems):
    rows, slots, tile = a_hbm.shape[0], a_hbm.shape[1], a_hbm.shape[2]
    columns = rows + 2 * HALO
    half = tile // 2
    copies = [pltpu.make_async_copy(a_hbm.at[t], a_ref.at[t], sems.at[t]) for t in range(rows)]
    for copy in copies:
        copy.start()
    acc_ref[...] = jnp.zeros_like(acc_ref)
    core = table_ref[0, 0] // CORE
    for r in range(rows):
        coarse = lax.rem(table_ref[r, 0], CORE) // columns
        for j in range(CG):
            place_ref[pl.ds(r * tile, tile), pl.ds(j * tile, tile)] = jnp.where(coarse == j, p_ref[r], jnp.zeros_like(p_ref[r]))
    for t in range(rows):
        p_t = p_ref[t].T
        copies[t].wait()
        for pair in range(slots // 2):
            both = jnp.concatenate([a_ref[t, 2 * pair], a_ref[t, 2 * pair + 1]], axis=1)
            terms = jnp.dot(p_t, both, preferred_element_type=jnp.float32)
            for side in range(2):
                at = lax.rem(table_ref[t, 2 * pair + side], CORE)
                acc_ref[at] += terms[:, side * tile : (side + 1) * tile]
    for i in range(CG):
        for part in range(2):
            first = pl.multiple_of((core if part == 1 else 1 - core) * half, half)
            to = pl.ds((part * CG + i) * half, half)
            for c in range(columns):
                block = acc_ref[i * columns + c, pl.ds(first, half), :].astype(jnp.bfloat16)
                if c < HALO:
                    g_ref[to, pl.ds(c * tile, tile)] = block
                elif c >= HALO + rows:
                    g_ref[to, pl.ds((c - rows) * tile, tile)] = block
                else:
                    gown_ref[to, pl.ds((c - HALO) * tile, tile)] = block
    own_ref[...] = jnp.dot(gown_ref[...], place_ref[...], preferred_element_type=jnp.float32).astype(jnp.bfloat16)


def back_kernel(g_ref, own_ref, before_ref, ahead_ref, out_ref, send_ref, place_ref):
    tile = before_ref.shape[2]
    rows = out_ref.shape[0]
    for side, halo_ref in enumerate((before_ref, ahead_ref)):
        for r in range(HALO):
            block = halo_ref[r, pl.ds(0, tile), :]
            mark = halo_ref[r, pl.ds(tile, MARK), :].astype(jnp.float32)[0:1, :]
            for j in range(CG):
                chosen = jnp.where(mark == float(j), 1.0, 0.0).astype(jnp.bfloat16)
                place_ref[side, pl.ds(r * tile, tile), pl.ds(j * tile, tile)] = block * chosen
    width = CG * tile
    for side in range(2):
        depth = HALO * tile
        result = jnp.dot(g_ref[:, pl.ds(side * depth, depth)], place_ref[side], preferred_element_type=jnp.float32).astype(jnp.bfloat16)
        at = pl.ds(2 * side * width, width)
        send_ref[:, at] = result[:rows]
        out_ref[:, at] = result[rows:]
    send_ref[:, pl.ds(width, width)] = own_ref[pl.ds(0, rows), :]
    out_ref[:, pl.ds(width, width)] = own_ref[pl.ds(rows, rows), :]


def local(groups, members, a_tiles, col_tiles, counts, aggregate, p_tiles):
    rows, slots, tile = a_tiles.shape[0], a_tiles.shape[1], a_tiles.shape[2]
    columns = rows + 2 * HALO
    coarse = lax.rem(aggregate, CG)
    marks = coarse.astype(jnp.bfloat16)

    def halo(first, step):
        inside = lax.broadcasted_iota(jnp.int32, (HALO, tile + MARK, tile), 1) < tile
        block = jnp.pad(p_tiles[first : first + HALO], ((0, 0), (0, MARK), (0, 0)))
        block = jnp.where(inside, block, marks[first : first + HALO, None, None])
        return lax.ppermute(block, "dom", [(i, (i + step) % groups) for i in range(groups)])

    before = halo(rows - HALO, 1)
    ahead = halo(0, -1)

    vmem = pl.BlockSpec(memory_space=pltpu.VMEM)
    side = lax.rem(col_tiles // (rows * members) - (lax.axis_index("dom") - 1 - groups), groups)
    near = coarse[:, None] * columns + lax.rem(col_tiles, rows) + rows * side - (rows - HALO)
    live = lax.broadcasted_iota(jnp.int32, col_tiles.shape, 1) < counts[:, None]
    table = jnp.clip(jnp.where(live, near, CG * columns), 0, CG * columns) + CORE * lax.rem(lax.axis_index("sub"), 2)

    g, own = pl.pallas_call(
        front_kernel,
        out_shape=(
            jax.ShapeDtypeStruct((CG * tile, 2 * HALO * tile), jnp.bfloat16),
            jax.ShapeDtypeStruct((CG * tile, CG * tile), jnp.bfloat16),
        ),
        in_specs=[pl.BlockSpec(memory_space=pltpu.SMEM), pl.BlockSpec(memory_space=pl.ANY), vmem],
        out_specs=(vmem, vmem),
        scratch_shapes=[
            pltpu.VMEM(a_tiles.shape, jnp.bfloat16),
            pltpu.VMEM((CG * columns + 1, tile, tile), jnp.float32),
            pltpu.VMEM((CG * tile, rows * tile), jnp.bfloat16),
            pltpu.VMEM((rows * tile, CG * tile), jnp.bfloat16),
            pltpu.SemaphoreType.DMA((rows,)),
        ],
        compiler_params=pltpu.CompilerParams(vmem_limit_bytes=52 * 2**20),
        cost_estimate=pl.CostEstimate(flops=2 * 10**9, bytes_accessed=4 * 2**20, transcendentals=0),
        name="front",
    )(table, a_tiles, p_tiles)

    share = CG * tile // 2
    keep, send = pl.pallas_call(
        back_kernel,
        out_shape=(jax.ShapeDtypeStruct((share, 3 * CG * tile), jnp.bfloat16),) * 2,
        in_specs=[vmem] * 4,
        out_specs=(vmem, vmem),
        scratch_shapes=[pltpu.VMEM((2, HALO * tile, CG * tile), jnp.bfloat16)],
        compiler_params=pltpu.CompilerParams(vmem_limit_bytes=24 * 2**20),
        cost_estimate=pl.CostEstimate(flops=3 * 10**8, bytes_accessed=3 * 2**20, transcendentals=0),
        name="back",
    )(g, own, before, ahead)
    other = lax.ppermute(send, "sub", [(i, i ^ 1) for i in range(members)])
    chip = (keep.astype(jnp.float32) + other.astype(jnp.float32)).astype(jnp.bfloat16)
    cores = [list(range(core, members, 2)) for core in range(2)]
    parts = lax.all_to_all(chip.reshape(members // 2, -1, chip.shape[1]), "sub", 0, 0, axis_index_groups=cores)
    return parts.astype(jnp.float32).sum(axis=0)


def solution(mesh):
    in_specs = (
        P(("dom", "sub"), None, None, None),
        P(("dom", "sub"), None),
        P(("dom", "sub")),
        P(("dom", "sub")),
        P(("dom", "sub"), None, None),
    )
    out_specs = P(("dom", "sub"), None)
    body = functools.partial(local, mesh.shape["dom"], mesh.shape["sub"])
    return jax.shard_map(body, mesh=mesh, in_specs=in_specs, out_specs=out_specs, check_vma=False)
```

```python
import functools

import jax
import jax.numpy as jnp
from jax import lax
from jax.experimental import pallas as pl
from jax.experimental.pallas import tpu as pltpu
from jax.sharding import PartitionSpec as P

CG = 4
HALO = 2
MARK = 16
CORE = 64


def front_kernel(table_ref, a_hbm, block_ref, g_ref, own_ref, a_ref, acc_ref, gown_ref, place_ref, pt_ref, sems):
    rows, slots, tile = a_hbm.shape[0], a_hbm.shape[1], a_hbm.shape[2]
    columns = rows + 2 * HALO
    half = tile // 2
    copies = [pltpu.make_async_copy(a_hbm.at[t], a_ref.at[t], sems.at[t]) for t in range(rows)]
    for copy in copies:
        copy.start()
    acc_ref[...] = jnp.zeros_like(acc_ref)
    core = table_ref[0, 0] // CORE
    for r in range(rows):
        coarse = lax.rem(table_ref[r, 0], CORE) // columns
        p_r = block_ref[r, pl.ds(0, tile), :]
        pt_ref[r] = p_r.T
        for j in range(CG):
            place_ref[pl.ds(r * tile, tile), pl.ds(j * tile, tile)] = jnp.where(coarse == j, p_r, jnp.zeros_like(p_r))
    for t in range(rows):
        if t % (rows // 2) == 0:
            for copy in copies[t : t + rows // 2]:
                copy.wait()
        for pair in range(slots // 2):
            both = jnp.concatenate([a_ref[t, 2 * pair], a_ref[t, 2 * pair + 1]], axis=1)
            terms = jnp.dot(pt_ref[t], both, preferred_element_type=jnp.float32)
            for side in range(2):
                at = lax.rem(table_ref[t, 2 * pair + side], CORE)
                acc_ref[at] += terms[:, side * tile : (side + 1) * tile]
    for i in range(CG):
        for part in range(2):
            first = pl.multiple_of((core if part == 1 else 1 - core) * half, half)
            to = pl.ds((part * CG + i) * half, half)
            for c in range(columns):
                block = acc_ref[i * columns + c, pl.ds(first, half), :].astype(jnp.bfloat16)
                if c < HALO:
                    g_ref[to, pl.ds(c * tile, tile)] = block
                elif c >= HALO + rows:
                    g_ref[to, pl.ds((c - rows) * tile, tile)] = block
                else:
                    gown_ref[to, pl.ds((c - HALO) * tile, tile)] = block
    own_ref[...] = jnp.dot(gown_ref[...], place_ref[...], preferred_element_type=jnp.float32).astype(jnp.bfloat16)


def back_kernel(g_ref, own_ref, first_ref, second_ref, out_ref, send_ref, place_ref):
    tile = first_ref.shape[2]
    rows = out_ref.shape[0]
    for r in range(HALO):
        tiles = [ref[r, pl.ds(0, tile), :] for ref in (first_ref, second_ref)]
        marks = [ref[r, pl.ds(tile, MARK), :].astype(jnp.float32)[0:1, :] for ref in (first_ref, second_ref)]
        for side in range(2):
            for j in range(CG):
                chosen = [jnp.where(mark == float(side * CG + j), 1.0, 0.0).astype(jnp.bfloat16) for mark in marks]
                place_ref[side, pl.ds(r * tile, tile), pl.ds(j * tile, tile)] = tiles[0] * chosen[0] + tiles[1] * chosen[1]
    width = CG * tile
    for side in range(2):
        depth = HALO * tile
        result = jnp.dot(g_ref[:, pl.ds(side * depth, depth)], place_ref[side], preferred_element_type=jnp.float32).astype(jnp.bfloat16)
        at = pl.ds(2 * side * width, width)
        send_ref[:, at] = result[:rows]
        out_ref[:, at] = result[rows:]
    send_ref[:, pl.ds(width, width)] = own_ref[pl.ds(0, rows), :]
    out_ref[:, pl.ds(width, width)] = own_ref[pl.ds(rows, rows), :]


def local(groups, members, a_tiles, col_tiles, counts, aggregate, p_tiles):
    rows, slots, tile = a_tiles.shape[0], a_tiles.shape[1], a_tiles.shape[2]
    columns = rows + 2 * HALO
    coarse = lax.rem(aggregate, CG)
    side = lax.rem(col_tiles // (rows * members) - (lax.axis_index("dom") - 1 - groups), groups)
    near = coarse[:, None] * columns + lax.rem(col_tiles, rows) + rows * side - (rows - HALO)
    live = lax.broadcasted_iota(jnp.int32, col_tiles.shape, 1) < counts[:, None]
    table = jnp.clip(jnp.where(live, near, CG * columns), 0, CG * columns) + CORE * lax.rem(lax.axis_index("sub"), 2)

    marks = coarse + jnp.where(lax.iota(jnp.int32, rows) < HALO, CG, 0)
    inside = lax.broadcasted_iota(jnp.int32, (rows, tile + MARK, tile), 1) < tile
    block = jnp.where(inside, jnp.pad(p_tiles, ((0, 0), (0, MARK), (0, 0))), marks.astype(jnp.bfloat16)[:, None, None])

    even = lax.rem(lax.axis_index("dom"), 2) == 0
    halos = []
    for turn in range(2):
        start = jnp.where(even == (turn == 0), rows - HALO, 0)
        route = []
        for i in range(turn, groups + turn, 2):
            route += [(i % groups, (i + 1) % groups), ((i + 1) % groups, i % groups)]
        halos.append(lax.ppermute(lax.dynamic_slice_in_dim(block, start, HALO), "dom", route))

    vmem = pl.BlockSpec(memory_space=pltpu.VMEM)
    g, own = pl.pallas_call(
        front_kernel,
        out_shape=(
            jax.ShapeDtypeStruct((CG * tile, 2 * HALO * tile), jnp.bfloat16),
            jax.ShapeDtypeStruct((CG * tile, CG * tile), jnp.bfloat16),
        ),
        in_specs=[pl.BlockSpec(memory_space=pltpu.SMEM), pl.BlockSpec(memory_space=pl.ANY), vmem],
        out_specs=(vmem, vmem),
        scratch_shapes=[
            pltpu.VMEM(a_tiles.shape, jnp.bfloat16),
            pltpu.VMEM((CG * columns + 1, tile, tile), jnp.float32),
            pltpu.VMEM((CG * tile, rows * tile), jnp.bfloat16),
            pltpu.VMEM((rows * tile, CG * tile), jnp.bfloat16),
            pltpu.VMEM(p_tiles.shape, jnp.bfloat16),
            pltpu.SemaphoreType.DMA((rows,)),
        ],
        compiler_params=pltpu.CompilerParams(vmem_limit_bytes=52 * 2**20),
        cost_estimate=pl.CostEstimate(flops=2 * 10**9, bytes_accessed=4 * 2**20, transcendentals=0),
        name="front",
    )(table, a_tiles, block)

    share = CG * tile // 2
    keep, send = pl.pallas_call(
        back_kernel,
        out_shape=(jax.ShapeDtypeStruct((share, 3 * CG * tile), jnp.bfloat16),) * 2,
        in_specs=[vmem] * 4,
        out_specs=(vmem, vmem),
        scratch_shapes=[pltpu.VMEM((2, HALO * tile, CG * tile), jnp.bfloat16)],
        compiler_params=pltpu.CompilerParams(vmem_limit_bytes=24 * 2**20),
        cost_estimate=pl.CostEstimate(flops=3 * 10**8, bytes_accessed=3 * 2**20, transcendentals=0),
        name="back",
    )(g, own, *halos)
    other = lax.ppermute(send, "sub", [(i, i ^ 1) for i in range(members)])
    chip = (keep.astype(jnp.float32) + other.astype(jnp.float32)).astype(jnp.bfloat16)
    cores = [list(range(core, members, 2)) for core in range(2)]
    parts = lax.all_to_all(chip.reshape(members // 2, -1, chip.shape[1]), "sub", 0, 0, axis_index_groups=cores)
    return parts.astype(jnp.float32).sum(axis=0)


def solution(mesh):
    in_specs = (
        P(("dom", "sub"), None, None, None),
        P(("dom", "sub"), None),
        P(("dom", "sub")),
        P(("dom", "sub")),
        P(("dom", "sub"), None, None),
    )
    out_specs = P(("dom", "sub"), None)
    body = functools.partial(local, mesh.shape["dom"], mesh.shape["sub"])
    return jax.shard_map(body, mesh=mesh, in_specs=in_specs, out_specs=out_specs, check_vma=False)
```

```python
import functools

import jax
import jax.numpy as jnp
from jax import lax
from jax.experimental import pallas as pl
from jax.experimental.pallas import tpu as pltpu
from jax.sharding import PartitionSpec as P

CG = 4
HALO = 2
MARK = 16


def pack_kernel(agg_hbm, p_hbm, first_ref, second_ref, agg_ref, ends_ref, sems):
    rows, tile = p_hbm.shape[0], p_hbm.shape[1]
    copies = [
        pltpu.make_async_copy(agg_hbm, agg_ref, sems.at[0]),
        pltpu.make_async_copy(p_hbm.at[pl.ds(0, HALO)], ends_ref.at[0], sems.at[1]),
        pltpu.make_async_copy(p_hbm.at[pl.ds(rows - HALO, HALO)], ends_ref.at[1], sems.at[2]),
    ]
    for copy in copies:
        copy.start()
    for copy in copies:
        copy.wait()
    odd = lax.rem(agg_ref[0] // CG, 2)
    for turn, ref in enumerate((first_ref, second_ref)):
        tail = 1 - odd if turn == 0 else odd
        for r in range(HALO):
            mark = lax.rem(agg_ref[tail * (rows - HALO) + r], CG) + (1 - tail) * CG
            ref[r, pl.ds(0, tile), :] = ends_ref[tail, r]
            ref[r, pl.ds(tile, MARK), :] = jnp.full((MARK, tile), mark.astype(jnp.float32)).astype(jnp.bfloat16)


def front_kernel(
    groups, members, col_hbm, count_hbm, agg_hbm, a_hbm, p_hbm, g_ref, own_ref,
    col_ref, count_ref, agg_ref, a_ref, p_ref, acc_ref, gown_ref, place_ref, pt_ref, sems, small_sems,
):
    rows, slots, tile = a_hbm.shape[0], a_hbm.shape[1], a_hbm.shape[2]
    columns = rows + 2 * HALO
    half = tile // 2
    copies = [pltpu.make_async_copy(a_hbm.at[t], a_ref.at[t], sems.at[t]) for t in range(rows)]
    pairs = ((col_hbm, col_ref), (count_hbm, count_ref), (agg_hbm, agg_ref), (p_hbm, p_ref))
    small = [pltpu.make_async_copy(source, to, small_sems.at[i]) for i, (source, to) in enumerate(pairs)]
    for copy in small + copies:
        copy.start()
    acc_ref[...] = jnp.zeros_like(acc_ref)
    for copy in small:
        copy.wait()
    device = col_ref[0, 0] // rows
    my_group = device // members
    core = lax.rem(device, 2)
    for r in range(rows):
        coarse = lax.rem(agg_ref[r], CG)
        p_r = p_ref[r]
        pt_ref[r] = p_r.T
        for j in range(CG):
            place_ref[pl.ds(r * tile, tile), pl.ds(j * tile, tile)] = jnp.where(coarse == j, p_r, jnp.zeros_like(p_r))
    for t in range(rows):
        if t % (rows // 2) == 0:
            for copy in copies[t : t + rows // 2]:
                copy.wait()
        for pair in range(slots // 2):
            both = jnp.concatenate([a_ref[t, 2 * pair], a_ref[t, 2 * pair + 1]], axis=1)
            terms = jnp.dot(pt_ref[t], both, preferred_element_type=jnp.float32)
            for side in range(2):
                k = 2 * pair + side
                column = col_ref[t, k]
                offset = lax.rem(column // (rows * members) - my_group + 1 + groups, groups)
                near = lax.rem(column, rows) + rows * offset - (rows - HALO)
                at = jnp.where(k < count_ref[t], lax.rem(agg_ref[t], CG) * columns + near, CG * columns)
                at = jnp.clip(at, 0, CG * columns)
                acc_ref[at] += terms[:, side * tile : (side + 1) * tile]
    for i in range(CG):
        for part in range(2):
            first = pl.multiple_of((core if part == 1 else 1 - core) * half, half)
            to = pl.ds((part * CG + i) * half, half)
            for c in range(columns):
                block = acc_ref[i * columns + c, pl.ds(first, half), :].astype(jnp.bfloat16)
                if c < HALO:
                    g_ref[to, pl.ds(c * tile, tile)] = block
                elif c >= HALO + rows:
                    g_ref[to, pl.ds((c - rows) * tile, tile)] = block
                else:
                    gown_ref[to, pl.ds((c - HALO) * tile, tile)] = block
    own_ref[...] = jnp.dot(gown_ref[...], place_ref[...], preferred_element_type=jnp.float32).astype(jnp.bfloat16)


def back_kernel(g_ref, own_ref, first_ref, second_ref, out_ref, send_ref, place_ref):
    tile = first_ref.shape[2]
    rows = out_ref.shape[0]
    for r in range(HALO):
        tiles = [ref[r, pl.ds(0, tile), :] for ref in (first_ref, second_ref)]
        marks = [ref[r, pl.ds(tile, MARK), :].astype(jnp.float32)[0:1, :] for ref in (first_ref, second_ref)]
        for side in range(2):
            for j in range(CG):
                chosen = [jnp.where(mark == float(side * CG + j), 1.0, 0.0).astype(jnp.bfloat16) for mark in marks]
                place_ref[side, pl.ds(r * tile, tile), pl.ds(j * tile, tile)] = tiles[0] * chosen[0] + tiles[1] * chosen[1]
    width = CG * tile
    for side in range(2):
        depth = HALO * tile
        result = jnp.dot(g_ref[:, pl.ds(side * depth, depth)], place_ref[side], preferred_element_type=jnp.float32).astype(jnp.bfloat16)
        at = pl.ds(2 * side * width, width)
        send_ref[:, at] = result[:rows]
        out_ref[:, at] = result[rows:]
    send_ref[:, pl.ds(width, width)] = own_ref[pl.ds(0, rows), :]
    out_ref[:, pl.ds(width, width)] = own_ref[pl.ds(rows, rows), :]


def local(groups, members, a_tiles, col_tiles, counts, aggregate, p_tiles):
    rows, slots, tile = a_tiles.shape[0], a_tiles.shape[1], a_tiles.shape[2]
    columns = rows + 2 * HALO
    hbm = pl.BlockSpec(memory_space=pltpu.HBM)
    keep_in_hbm = functools.partial(pltpu.with_memory_space_constraint, memory_space=pltpu.HBM)
    a_tiles, col_tiles, counts, aggregate, p_tiles = map(keep_in_hbm, (a_tiles, col_tiles, counts, aggregate, p_tiles))
    vmem = pl.BlockSpec(memory_space=pltpu.VMEM)
    blocks = pl.pallas_call(
        pack_kernel,
        out_shape=(jax.ShapeDtypeStruct((HALO, tile + MARK, tile), jnp.bfloat16),) * 2,
        in_specs=[hbm, hbm],
        out_specs=(vmem, vmem),
        scratch_shapes=[
            pltpu.SMEM(aggregate.shape, jnp.int32),
            pltpu.VMEM((2, HALO, tile, tile), jnp.bfloat16),
            pltpu.SemaphoreType.DMA((3,)),
        ],
        name="pack",
    )(aggregate, p_tiles)
    halos = []
    for turn, block in enumerate(blocks):
        route = []
        for i in range(turn, groups + turn, 2):
            route += [(i % groups, (i + 1) % groups), ((i + 1) % groups, i % groups)]
        halos.append(lax.ppermute(block, "dom", route))

    g, own = pl.pallas_call(
        functools.partial(front_kernel, groups, members),
        out_shape=(
            jax.ShapeDtypeStruct((CG * tile, 2 * HALO * tile), jnp.bfloat16),
            jax.ShapeDtypeStruct((CG * tile, CG * tile), jnp.bfloat16),
        ),
        in_specs=[hbm] * 5,
        out_specs=(vmem, vmem),
        scratch_shapes=[
            pltpu.SMEM(col_tiles.shape, jnp.int32),
            pltpu.SMEM(counts.shape, jnp.int32),
            pltpu.SMEM(aggregate.shape, jnp.int32),
            pltpu.VMEM(a_tiles.shape, jnp.bfloat16),
            pltpu.VMEM(p_tiles.shape, jnp.bfloat16),
            pltpu.VMEM((CG * columns + 1, tile, tile), jnp.float32),
            pltpu.VMEM((CG * tile, rows * tile), jnp.bfloat16),
            pltpu.VMEM((rows * tile, CG * tile), jnp.bfloat16),
            pltpu.VMEM(p_tiles.shape, jnp.bfloat16),
            pltpu.SemaphoreType.DMA((rows,)),
            pltpu.SemaphoreType.DMA((4,)),
        ],
        compiler_params=pltpu.CompilerParams(vmem_limit_bytes=24 * 2**20),
        cost_estimate=pl.CostEstimate(flops=2 * 10**9, bytes_accessed=4 * 2**20, transcendentals=0),
        name="front",
    )(col_tiles, counts, aggregate, a_tiles, p_tiles)

    share = CG * tile // 2
    keep, send = pl.pallas_call(
        back_kernel,
        out_shape=(jax.ShapeDtypeStruct((share, 3 * CG * tile), jnp.bfloat16),) * 2,
        in_specs=[vmem] * 4,
        out_specs=(vmem, vmem),
        scratch_shapes=[pltpu.VMEM((2, HALO * tile, CG * tile), jnp.bfloat16)],
        compiler_params=pltpu.CompilerParams(vmem_limit_bytes=24 * 2**20),
        cost_estimate=pl.CostEstimate(flops=3 * 10**8, bytes_accessed=3 * 2**20, transcendentals=0),
        name="back",
    )(g, own, *halos)
    other = lax.ppermute(send, "sub", [(i, i ^ 1) for i in range(members)])
    chip = (keep.astype(jnp.float32) + other.astype(jnp.float32)).astype(jnp.bfloat16)
    cores = [list(range(core, members, 2)) for core in range(2)]
    parts = lax.all_to_all(chip.reshape(members // 2, -1, chip.shape[1]), "sub", 0, 0, axis_index_groups=cores)
    return parts.astype(jnp.float32).sum(axis=0)


def solution(mesh):
    in_specs = (
        P(("dom", "sub"), None, None, None),
        P(("dom", "sub"), None),
        P(("dom", "sub")),
        P(("dom", "sub")),
        P(("dom", "sub"), None, None),
    )
    out_specs = P(("dom", "sub"), None)
    body = functools.partial(local, mesh.shape["dom"], mesh.shape["sub"])
    return jax.shard_map(body, mesh=mesh, in_specs=in_specs, out_specs=out_specs, check_vma=False)
```

```python
import functools

import jax
import jax.numpy as jnp
from jax import lax
from jax.experimental import pallas as pl
from jax.experimental.pallas import tpu as pltpu
from jax.sharding import PartitionSpec as P

CG = 4
HALO = 2
TURNS = ((3, 1, 2), (1, 3, 2))
MARK = 16


def pack_kernel(agg_hbm, p_hbm, first_ref, second_ref, agg_ref, ends_ref, sems):
    rows, tile = p_hbm.shape[0], p_hbm.shape[1]
    copies = [
        pltpu.make_async_copy(agg_hbm, agg_ref, sems.at[0]),
        pltpu.make_async_copy(p_hbm.at[pl.ds(0, HALO)], ends_ref.at[0], sems.at[1]),
        pltpu.make_async_copy(p_hbm.at[pl.ds(rows - HALO, HALO)], ends_ref.at[1], sems.at[2]),
    ]
    for copy in copies:
        copy.start()
    for copy in copies:
        copy.wait()
    odd = lax.rem(agg_ref[0] // CG, 2)
    for turn, ref in enumerate((first_ref, second_ref)):
        tail = odd if turn == 0 else 1 - odd
        for r in range(HALO):
            mark = lax.rem(agg_ref[tail * (rows - HALO) + r], CG) + (1 - tail) * CG
            ref[r, pl.ds(0, tile), :] = ends_ref[tail, r]
            ref[r, pl.ds(tile, MARK), :] = jnp.full((MARK, tile), mark.astype(jnp.float32)).astype(jnp.bfloat16)


def turn_of(apart, core):
    place = 0
    for turn, step in enumerate(TURNS[core], start=1):
        place = jnp.where(apart == step, turn, place)
    return place


def front_kernel(
    groups, members, col_hbm, count_hbm, agg_hbm, a_hbm, p_hbm, g_ref, own_ref,
    col_ref, count_ref, agg_ref, a_ref, p_ref, acc_ref, gown_ref, place_ref, pt_ref, sems, small_sems,
):
    rows, slots, tile = a_hbm.shape[0], a_hbm.shape[1], a_hbm.shape[2]
    columns = rows + 2 * HALO
    half = tile // 2
    copies = [pltpu.make_async_copy(a_hbm.at[t], a_ref.at[t], sems.at[t]) for t in range(rows)]
    pairs = ((col_hbm, col_ref), (count_hbm, count_ref), (agg_hbm, agg_ref), (p_hbm, p_ref))
    small = [pltpu.make_async_copy(source, to, small_sems.at[i]) for i, (source, to) in enumerate(pairs)]
    for copy in small + copies:
        copy.start()
    acc_ref[...] = jnp.zeros_like(acc_ref)
    for copy in small:
        copy.wait()
    device = col_ref[0, 0] // rows
    my_group = device // members
    core = lax.rem(device, 2)
    chip = lax.rem(device, members) // 2
    for r in range(rows):
        coarse = lax.rem(agg_ref[r], CG)
        p_r = p_ref[r]
        pt_ref[r] = p_r.T
        for j in range(CG):
            place_ref[pl.ds(r * tile, tile), pl.ds(j * tile, tile)] = jnp.where(coarse == j, p_r, jnp.zeros_like(p_r))
    for t in range(rows):
        if t % (rows // 2) == 0:
            for copy in copies[t : t + rows // 2]:
                copy.wait()
        for pair in range(slots // 2):
            both = jnp.concatenate([a_ref[t, 2 * pair], a_ref[t, 2 * pair + 1]], axis=1)
            terms = jnp.dot(pt_ref[t], both, preferred_element_type=jnp.float32)
            for side in range(2):
                k = 2 * pair + side
                column = col_ref[t, k]
                offset = lax.rem(column // (rows * members) - my_group + 1 + groups, groups)
                near = lax.rem(column, rows) + rows * offset - (rows - HALO)
                at = jnp.where(k < count_ref[t], lax.rem(agg_ref[t], CG) * columns + near, CG * columns)
                at = jnp.clip(at, 0, CG * columns)
                acc_ref[at] += terms[:, side * tile : (side + 1) * tile]
    for i in range(CG):
        for part in range(2):
            first = pl.multiple_of((core if part == 1 else 1 - core) * half, half)
            turn = jnp.where(core == 1 - part, turn_of(i ^ chip, 0), turn_of(i ^ chip, 1))
            to = pl.ds(pl.multiple_of((part * CG + turn) * half, half), half)
            for c in range(columns):
                block = acc_ref[i * columns + c, pl.ds(first, half), :].astype(jnp.bfloat16)
                if c < HALO:
                    g_ref[to, pl.ds(c * tile, tile)] = block
                elif c >= HALO + rows:
                    g_ref[to, pl.ds((c - rows) * tile, tile)] = block
                else:
                    gown_ref[to, pl.ds((c - HALO) * tile, tile)] = block
    own_ref[...] = jnp.dot(gown_ref[...], place_ref[...], preferred_element_type=jnp.float32).astype(jnp.bfloat16)


def back_kernel(g_ref, own_ref, first_ref, second_ref, out_ref, send_ref, place_ref):
    tile = first_ref.shape[2]
    rows = out_ref.shape[0]
    for r in range(HALO):
        tiles = [ref[r, pl.ds(0, tile), :] for ref in (first_ref, second_ref)]
        marks = [ref[r, pl.ds(tile, MARK), :].astype(jnp.float32)[0:1, :] for ref in (first_ref, second_ref)]
        for side in range(2):
            for j in range(CG):
                chosen = [jnp.where(mark == float(side * CG + j), 1.0, 0.0).astype(jnp.bfloat16) for mark in marks]
                place_ref[side, pl.ds(r * tile, tile), pl.ds(j * tile, tile)] = tiles[0] * chosen[0] + tiles[1] * chosen[1]
    width = CG * tile
    for side in range(2):
        depth = HALO * tile
        result = jnp.dot(g_ref[:, pl.ds(side * depth, depth)], place_ref[side], preferred_element_type=jnp.float32).astype(jnp.bfloat16)
        at = pl.ds(2 * side * width, width)
        send_ref[:, at] = result[:rows]
        out_ref[:, at] = result[rows:]
    send_ref[:, pl.ds(width, width)] = own_ref[pl.ds(0, rows), :]
    out_ref[:, pl.ds(width, width)] = own_ref[pl.ds(rows, rows), :]


def local(groups, members, a_tiles, col_tiles, counts, aggregate, p_tiles):
    rows, slots, tile = a_tiles.shape[0], a_tiles.shape[1], a_tiles.shape[2]
    columns = rows + 2 * HALO
    hbm = pl.BlockSpec(memory_space=pltpu.HBM)
    keep_in_hbm = functools.partial(pltpu.with_memory_space_constraint, memory_space=pltpu.HBM)
    a_tiles, col_tiles, counts, aggregate, p_tiles = map(keep_in_hbm, (a_tiles, col_tiles, counts, aggregate, p_tiles))
    vmem = pl.BlockSpec(memory_space=pltpu.VMEM)
    blocks = pl.pallas_call(
        pack_kernel,
        out_shape=(jax.ShapeDtypeStruct((HALO, tile + MARK, tile), jnp.bfloat16),) * 2,
        in_specs=[hbm, hbm],
        out_specs=(vmem, vmem),
        scratch_shapes=[
            pltpu.SMEM(aggregate.shape, jnp.int32),
            pltpu.VMEM((2, HALO, tile, tile), jnp.bfloat16),
            pltpu.SemaphoreType.DMA((3,)),
        ],
        name="pack",
    )(aggregate, p_tiles)
    halos = []
    for turn, block in enumerate(blocks):
        route = []
        for i in range(1 - turn, groups + 1 - turn, 2):
            route += [(i % groups, (i + 1) % groups), ((i + 1) % groups, i % groups)]
        halos.append(lax.ppermute(block, "dom", route))

    g, own = pl.pallas_call(
        functools.partial(front_kernel, groups, members),
        out_shape=(
            jax.ShapeDtypeStruct((CG * tile, 2 * HALO * tile), jnp.bfloat16),
            jax.ShapeDtypeStruct((CG * tile, CG * tile), jnp.bfloat16),
        ),
        in_specs=[hbm] * 5,
        out_specs=(vmem, vmem),
        scratch_shapes=[
            pltpu.SMEM(col_tiles.shape, jnp.int32),
            pltpu.SMEM(counts.shape, jnp.int32),
            pltpu.SMEM(aggregate.shape, jnp.int32),
            pltpu.VMEM(a_tiles.shape, jnp.bfloat16),
            pltpu.VMEM(p_tiles.shape, jnp.bfloat16),
            pltpu.VMEM((CG * columns + 1, tile, tile), jnp.float32),
            pltpu.VMEM((CG * tile, rows * tile), jnp.bfloat16),
            pltpu.VMEM((rows * tile, CG * tile), jnp.bfloat16),
            pltpu.VMEM(p_tiles.shape, jnp.bfloat16),
            pltpu.SemaphoreType.DMA((rows,)),
            pltpu.SemaphoreType.DMA((4,)),
        ],
        compiler_params=pltpu.CompilerParams(vmem_limit_bytes=24 * 2**20),
        cost_estimate=pl.CostEstimate(flops=2 * 10**9, bytes_accessed=4 * 2**20, transcendentals=0),
        name="front",
    )(col_tiles, counts, aggregate, a_tiles, p_tiles)

    share = CG * tile // 2
    keep, send = pl.pallas_call(
        back_kernel,
        out_shape=(jax.ShapeDtypeStruct((share, 3 * CG * tile), jnp.bfloat16),) * 2,
        in_specs=[vmem] * 4,
        out_specs=(vmem, vmem),
        scratch_shapes=[pltpu.VMEM((2, HALO * tile, CG * tile), jnp.bfloat16)],
        compiler_params=pltpu.CompilerParams(vmem_limit_bytes=24 * 2**20),
        cost_estimate=pl.CostEstimate(flops=3 * 10**8, bytes_accessed=3 * 2**20, transcendentals=0),
        name="back",
    )(g, own, *halos)
    other = lax.ppermute(send, "sub", [(i, i ^ 1) for i in range(members)])
    chip = (keep.astype(jnp.float32) + other.astype(jnp.float32)).astype(jnp.bfloat16)
    parts = chip.reshape(members // 2, -1, chip.shape[1])
    total = parts[0].astype(jnp.float32)
    for turn in range(1, members // 2):
        route = [(i, i ^ (2 * TURNS[i % 2][turn - 1])) for i in range(members)]
        total += lax.ppermute(parts[turn], "sub", route).astype(jnp.float32)
    return total


def solution(mesh):
    in_specs = (
        P(("dom", "sub"), None, None, None),
        P(("dom", "sub"), None),
        P(("dom", "sub")),
        P(("dom", "sub")),
        P(("dom", "sub"), None, None),
    )
    out_specs = P(("dom", "sub"), None)
    body = functools.partial(local, mesh.shape["dom"], mesh.shape["sub"])
    return jax.shard_map(body, mesh=mesh, in_specs=in_specs, out_specs=out_specs, check_vma=False)
```

```python
import functools

import jax
import jax.numpy as jnp
from jax import lax
from jax.experimental import pallas as pl
from jax.experimental.pallas import tpu as pltpu
from jax.sharding import PartitionSpec as P

CG = 4
HALO = 2
TURNS = ((2, 1, 3), (3, 1, 2))
MARK = 16


def pack_kernel(agg_hbm, p_hbm, first_ref, second_ref, agg_ref, ends_ref, sems):
    rows, tile = p_hbm.shape[0], p_hbm.shape[1]
    copies = [
        pltpu.make_async_copy(agg_hbm, agg_ref, sems.at[0]),
        pltpu.make_async_copy(p_hbm.at[pl.ds(0, HALO)], ends_ref.at[0], sems.at[1]),
        pltpu.make_async_copy(p_hbm.at[pl.ds(rows - HALO, HALO)], ends_ref.at[1], sems.at[2]),
    ]
    for copy in copies:
        copy.start()
    for copy in copies:
        copy.wait()
    odd = lax.rem(agg_ref[0] // CG, 2)
    for turn, ref in enumerate((first_ref, second_ref)):
        tail = odd if turn == 0 else 1 - odd
        for r in range(HALO):
            mark = lax.rem(agg_ref[tail * (rows - HALO) + r], CG) + (1 - tail) * CG
            ref[r, pl.ds(0, tile), :] = ends_ref[tail, r]
            ref[r, pl.ds(tile, MARK), :] = jnp.full((MARK, tile), mark.astype(jnp.float32)).astype(jnp.bfloat16)


def turn_of(apart, core):
    place = 0
    for turn, step in enumerate(TURNS[core], start=1):
        place = jnp.where(apart == step, turn, place)
    return place


def front_kernel(
    groups, members, col_hbm, count_hbm, agg_hbm, a_hbm, p_hbm, g_ref, own_ref,
    col_ref, count_ref, agg_ref, a_ref, p_ref, acc_ref, gown_ref, place_ref, pt_ref, sems, small_sems,
):
    rows, slots, tile = a_hbm.shape[0], a_hbm.shape[1], a_hbm.shape[2]
    columns = rows + 2 * HALO
    half = tile // 2
    copies = [pltpu.make_async_copy(a_hbm.at[t], a_ref.at[t], sems.at[t]) for t in range(rows)]
    pairs = ((col_hbm, col_ref), (count_hbm, count_ref), (agg_hbm, agg_ref), (p_hbm, p_ref))
    small = [pltpu.make_async_copy(source, to, small_sems.at[i]) for i, (source, to) in enumerate(pairs)]
    for copy in small + copies:
        copy.start()
    acc_ref[...] = jnp.zeros_like(acc_ref)
    for copy in small:
        copy.wait()
    device = col_ref[0, 0] // rows
    my_group = device // members
    core = lax.rem(device, 2)
    chip = lax.rem(device, members) // 2
    for r in range(rows):
        coarse = lax.rem(agg_ref[r], CG)
        p_r = p_ref[r]
        pt_ref[r] = p_r.T
        for j in range(CG):
            place_ref[pl.ds(r * tile, tile), pl.ds(j * tile, tile)] = jnp.where(coarse == j, p_r, jnp.zeros_like(p_r))
    for t in range(rows):
        if t % (rows // 2) == 0:
            for copy in copies[t : t + rows // 2]:
                copy.wait()
        for pair in range(slots // 2):
            both = jnp.concatenate([a_ref[t, 2 * pair], a_ref[t, 2 * pair + 1]], axis=1)
            terms = jnp.dot(pt_ref[t], both, preferred_element_type=jnp.float32)
            for side in range(2):
                k = 2 * pair + side
                column = col_ref[t, k]
                offset = lax.rem(column // (rows * members) - my_group + 1 + groups, groups)
                near = lax.rem(column, rows) + rows * offset - (rows - HALO)
                at = jnp.where(k < count_ref[t], lax.rem(agg_ref[t], CG) * columns + near, CG * columns)
                at = jnp.clip(at, 0, CG * columns)
                acc_ref[at] += terms[:, side * tile : (side + 1) * tile]
    for i in range(CG):
        for part in range(2):
            first = pl.multiple_of((core if part == 1 else 1 - core) * half, half)
            turn = jnp.where(core == 1 - part, turn_of(i ^ chip, 0), turn_of(i ^ chip, 1))
            to = pl.ds(pl.multiple_of((part * CG + turn) * half, half), half)
            for c in range(columns):
                block = acc_ref[i * columns + c, pl.ds(first, half), :].astype(jnp.bfloat16)
                if c < HALO:
                    g_ref[to, pl.ds(c * tile, tile)] = block
                elif c >= HALO + rows:
                    g_ref[to, pl.ds((c - rows) * tile, tile)] = block
                else:
                    gown_ref[to, pl.ds((c - HALO) * tile, tile)] = block
    own_ref[...] = jnp.dot(gown_ref[...], place_ref[...], preferred_element_type=jnp.float32).astype(jnp.bfloat16)


def back_kernel(g_ref, own_ref, first_ref, second_ref, out_ref, send_ref, place_ref):
    tile = first_ref.shape[2]
    rows = out_ref.shape[0]
    for r in range(HALO):
        tiles = [ref[r, pl.ds(0, tile), :] for ref in (first_ref, second_ref)]
        marks = [ref[r, pl.ds(tile, MARK), :].astype(jnp.float32)[0:1, :] for ref in (first_ref, second_ref)]
        for side in range(2):
            for j in range(CG):
                chosen = [jnp.where(mark == float(side * CG + j), 1.0, 0.0).astype(jnp.bfloat16) for mark in marks]
                place_ref[side, pl.ds(r * tile, tile), pl.ds(j * tile, tile)] = tiles[0] * chosen[0] + tiles[1] * chosen[1]
    width = CG * tile
    for side in range(2):
        depth = HALO * tile
        result = jnp.dot(g_ref[:, pl.ds(side * depth, depth)], place_ref[side], preferred_element_type=jnp.float32).astype(jnp.bfloat16)
        at = pl.ds(2 * side * width, width)
        send_ref[:, at] = result[:rows]
        out_ref[:, at] = result[rows:]
    send_ref[:, pl.ds(width, width)] = own_ref[pl.ds(0, rows), :]
    out_ref[:, pl.ds(width, width)] = own_ref[pl.ds(rows, rows), :]


def local(groups, members, a_tiles, col_tiles, counts, aggregate, p_tiles):
    rows, slots, tile = a_tiles.shape[0], a_tiles.shape[1], a_tiles.shape[2]
    columns = rows + 2 * HALO
    hbm = pl.BlockSpec(memory_space=pltpu.HBM)
    keep_in_hbm = functools.partial(pltpu.with_memory_space_constraint, memory_space=pltpu.HBM)
    a_tiles, col_tiles, counts, aggregate, p_tiles = map(keep_in_hbm, (a_tiles, col_tiles, counts, aggregate, p_tiles))
    vmem = pl.BlockSpec(memory_space=pltpu.VMEM)
    blocks = pl.pallas_call(
        pack_kernel,
        out_shape=(jax.ShapeDtypeStruct((HALO, tile + MARK, tile), jnp.bfloat16),) * 2,
        in_specs=[hbm, hbm],
        out_specs=(vmem, vmem),
        scratch_shapes=[
            pltpu.SMEM(aggregate.shape, jnp.int32),
            pltpu.VMEM((2, HALO, tile, tile), jnp.bfloat16),
            pltpu.SemaphoreType.DMA((3,)),
        ],
        name="pack",
    )(aggregate, p_tiles)
    halos = []
    for turn, block in enumerate(blocks):
        route = []
        for i in range(1 - turn, groups + 1 - turn, 2):
            route += [(i % groups, (i + 1) % groups), ((i + 1) % groups, i % groups)]
        halos.append(lax.ppermute(block, "dom", route))

    g, own = pl.pallas_call(
        functools.partial(front_kernel, groups, members),
        out_shape=(
            jax.ShapeDtypeStruct((CG * tile, 2 * HALO * tile), jnp.bfloat16),
            jax.ShapeDtypeStruct((CG * tile, CG * tile), jnp.bfloat16),
        ),
        in_specs=[hbm] * 5,
        out_specs=(vmem, vmem),
        scratch_shapes=[
            pltpu.SMEM(col_tiles.shape, jnp.int32),
            pltpu.SMEM(counts.shape, jnp.int32),
            pltpu.SMEM(aggregate.shape, jnp.int32),
            pltpu.VMEM(a_tiles.shape, jnp.bfloat16),
            pltpu.VMEM(p_tiles.shape, jnp.bfloat16),
            pltpu.VMEM((CG * columns + 1, tile, tile), jnp.float32),
            pltpu.VMEM((CG * tile, rows * tile), jnp.bfloat16),
            pltpu.VMEM((rows * tile, CG * tile), jnp.bfloat16),
            pltpu.VMEM(p_tiles.shape, jnp.bfloat16),
            pltpu.SemaphoreType.DMA((rows,)),
            pltpu.SemaphoreType.DMA((4,)),
        ],
        compiler_params=pltpu.CompilerParams(vmem_limit_bytes=24 * 2**20),
        cost_estimate=pl.CostEstimate(flops=2 * 10**9, bytes_accessed=4 * 2**20, transcendentals=0),
        name="front",
    )(col_tiles, counts, aggregate, a_tiles, p_tiles)

    share = CG * tile // 2
    keep, send = pl.pallas_call(
        back_kernel,
        out_shape=(jax.ShapeDtypeStruct((share, 3 * CG * tile), jnp.bfloat16),) * 2,
        in_specs=[vmem] * 4,
        out_specs=(vmem, vmem),
        scratch_shapes=[pltpu.VMEM((2, HALO * tile, CG * tile), jnp.bfloat16)],
        compiler_params=pltpu.CompilerParams(vmem_limit_bytes=24 * 2**20),
        cost_estimate=pl.CostEstimate(flops=3 * 10**8, bytes_accessed=3 * 2**20, transcendentals=0),
        name="back",
    )(g, own, *halos)
    other = lax.ppermute(send, "sub", [(i, i ^ 1) for i in range(members)])
    chip = (keep.astype(jnp.float32) + other.astype(jnp.float32)).astype(jnp.bfloat16)
    parts = chip.reshape(members // 2, -1, chip.shape[1])
    total = parts[0].astype(jnp.float32)
    for turn in range(1, members // 2):
        route = [(i, i ^ (2 * TURNS[i % 2][turn - 1])) for i in range(members)]
        total += lax.ppermute(parts[turn], "sub", route).astype(jnp.float32)
    return total


def solution(mesh):
    in_specs = (
        P(("dom", "sub"), None, None, None),
        P(("dom", "sub"), None),
        P(("dom", "sub")),
        P(("dom", "sub")),
        P(("dom", "sub"), None, None),
    )
    out_specs = P(("dom", "sub"), None)
    body = functools.partial(local, mesh.shape["dom"], mesh.shape["sub"])
    return jax.shard_map(body, mesh=mesh, in_specs=in_specs, out_specs=out_specs, check_vma=False)
```

```python
import functools

import jax
import jax.numpy as jnp
from jax import lax
from jax.experimental import pallas as pl
from jax.experimental.pallas import tpu as pltpu
from jax.sharding import PartitionSpec as P

CG = 4
HALO = 2
TURNS = ((2, 1, 3), (3, 1, 2))
MARK = 16


def pack_kernel(agg_hbm, p_hbm, first_ref, second_ref, agg_ref, ends_ref, sems):
    rows, tile = p_hbm.shape[0], p_hbm.shape[1]
    copies = [
        pltpu.make_async_copy(agg_hbm, agg_ref, sems.at[0]),
        pltpu.make_async_copy(p_hbm.at[pl.ds(0, HALO)], ends_ref.at[0], sems.at[1]),
        pltpu.make_async_copy(p_hbm.at[pl.ds(rows - HALO, HALO)], ends_ref.at[1], sems.at[2]),
    ]
    for copy in copies:
        copy.start()
    for copy in copies:
        copy.wait()
    odd = lax.rem(agg_ref[0] // CG, 2)
    for turn, ref in enumerate((first_ref, second_ref)):
        tail = 1 - odd if turn == 0 else odd
        for r in range(HALO):
            mark = lax.rem(agg_ref[tail * (rows - HALO) + r], CG) + (1 - tail) * CG
            ref[r, pl.ds(0, tile), :] = ends_ref[tail, r]
            ref[r, pl.ds(tile, MARK), :] = jnp.full((MARK, tile), mark.astype(jnp.float32)).astype(jnp.bfloat16)


def turn_of(apart, core):
    place = 0
    for turn, step in enumerate(TURNS[core], start=1):
        place = jnp.where(apart == step, turn, place)
    return place


def front_kernel(
    groups, members, col_ref, count_ref, agg_ref, a_ref, p_ref, g_ref, own_ref, acc_ref, gown_ref, place_ref, pt_ref
):
    rows, slots, tile = a_ref.shape[0], a_ref.shape[1], a_ref.shape[2]
    columns = rows + 2 * HALO
    half = tile // 2
    acc_ref[...] = jnp.zeros_like(acc_ref)
    device = col_ref[0, 0] // rows
    my_group = device // members
    core = lax.rem(device, 2)
    chip = lax.rem(device, members) // 2
    for r in range(rows):
        coarse = lax.rem(agg_ref[r], CG)
        p_r = p_ref[r]
        pt_ref[r] = p_r.T
        for j in range(CG):
            place_ref[pl.ds(r * tile, tile), pl.ds(j * tile, tile)] = jnp.where(coarse == j, p_r, jnp.zeros_like(p_r))
    for t in range(rows):
        for pair in range(slots // 2):
            both = jnp.concatenate([a_ref[t, 2 * pair], a_ref[t, 2 * pair + 1]], axis=1)
            terms = jnp.dot(pt_ref[t], both, preferred_element_type=jnp.float32)
            for side in range(2):
                k = 2 * pair + side
                column = col_ref[t, k]
                offset = lax.rem(column // (rows * members) - my_group + 1 + groups, groups)
                near = lax.rem(column, rows) + rows * offset - (rows - HALO)
                at = jnp.where(k < count_ref[t], lax.rem(agg_ref[t], CG) * columns + near, CG * columns)
                at = jnp.clip(at, 0, CG * columns)
                acc_ref[at] += terms[:, side * tile : (side + 1) * tile]
    for i in range(CG):
        for part in range(2):
            first = pl.multiple_of((core if part == 1 else 1 - core) * half, half)
            turn = jnp.where(core == 1 - part, turn_of(i ^ chip, 0), turn_of(i ^ chip, 1))
            to = pl.ds(pl.multiple_of((part * CG + turn) * half, half), half)
            for c in range(columns):
                block = acc_ref[i * columns + c, pl.ds(first, half), :].astype(jnp.bfloat16)
                if c < HALO:
                    g_ref[to, pl.ds(c * tile, tile)] = block
                elif c >= HALO + rows:
                    g_ref[to, pl.ds((c - rows) * tile, tile)] = block
                else:
                    gown_ref[to, pl.ds((c - HALO) * tile, tile)] = block
    own_ref[...] = jnp.dot(gown_ref[...], place_ref[...], preferred_element_type=jnp.float32).astype(jnp.bfloat16)


def back_kernel(g_ref, own_ref, first_ref, second_ref, out_ref, send_ref, place_ref):
    tile = first_ref.shape[2]
    rows = out_ref.shape[0]
    for r in range(HALO):
        tiles = [ref[r, pl.ds(0, tile), :] for ref in (first_ref, second_ref)]
        marks = [ref[r, pl.ds(tile, MARK), :].astype(jnp.float32)[0:1, :] for ref in (first_ref, second_ref)]
        for side in range(2):
            for j in range(CG):
                chosen = [jnp.where(mark == float(side * CG + j), 1.0, 0.0).astype(jnp.bfloat16) for mark in marks]
                place_ref[side, pl.ds(r * tile, tile), pl.ds(j * tile, tile)] = tiles[0] * chosen[0] + tiles[1] * chosen[1]
    width = CG * tile
    for side in range(2):
        depth = HALO * tile
        result = jnp.dot(g_ref[:, pl.ds(side * depth, depth)], place_ref[side], preferred_element_type=jnp.float32).astype(jnp.bfloat16)
        at = pl.ds(2 * side * width, width)
        send_ref[:, at] = result[:rows]
        out_ref[:, at] = result[rows:]
    send_ref[:, pl.ds(width, width)] = own_ref[pl.ds(0, rows), :]
    out_ref[:, pl.ds(width, width)] = own_ref[pl.ds(rows, rows), :]


def local(groups, members, a_tiles, col_tiles, counts, aggregate, p_tiles):
    rows, slots, tile = a_tiles.shape[0], a_tiles.shape[1], a_tiles.shape[2]
    columns = rows + 2 * HALO
    hbm = pl.BlockSpec(memory_space=pltpu.HBM)
    smem = pl.BlockSpec(memory_space=pltpu.SMEM)
    keep_in_hbm = functools.partial(pltpu.with_memory_space_constraint, memory_space=pltpu.HBM)
    vmem = pl.BlockSpec(memory_space=pltpu.VMEM)
    blocks = pl.pallas_call(
        pack_kernel,
        out_shape=(jax.ShapeDtypeStruct((HALO, tile + MARK, tile), jnp.bfloat16),) * 2,
        in_specs=[hbm, hbm],
        out_specs=(vmem, vmem),
        scratch_shapes=[
            pltpu.SMEM(aggregate.shape, jnp.int32),
            pltpu.VMEM((2, HALO, tile, tile), jnp.bfloat16),
            pltpu.SemaphoreType.DMA((3,)),
        ],
        cost_estimate=pl.CostEstimate(flops=10**9, bytes_accessed=64 * 2**20, transcendentals=0),
        name="pack",
    )(keep_in_hbm(aggregate), keep_in_hbm(p_tiles))
    halos = []
    for turn, block in enumerate(blocks):
        route = []
        for i in range(turn, groups + turn, 2):
            route += [(i % groups, (i + 1) % groups), ((i + 1) % groups, i % groups)]
        halos.append(lax.ppermute(block, "dom", route))

    g, own = pl.pallas_call(
        functools.partial(front_kernel, groups, members),
        out_shape=(
            jax.ShapeDtypeStruct((CG * tile, 2 * HALO * tile), jnp.bfloat16),
            jax.ShapeDtypeStruct((CG * tile, CG * tile), jnp.bfloat16),
        ),
        in_specs=[smem] * 3 + [vmem] * 2,
        out_specs=(vmem, vmem),
        scratch_shapes=[
            pltpu.VMEM((CG * columns + 1, tile, tile), jnp.float32),
            pltpu.VMEM((CG * tile, rows * tile), jnp.bfloat16),
            pltpu.VMEM((rows * tile, CG * tile), jnp.bfloat16),
            pltpu.VMEM(p_tiles.shape, jnp.bfloat16),
        ],
        compiler_params=pltpu.CompilerParams(vmem_limit_bytes=24 * 2**20),
        cost_estimate=pl.CostEstimate(flops=2 * 10**9, bytes_accessed=4 * 2**20, transcendentals=0),
        name="front",
    )(col_tiles, counts, aggregate, a_tiles, p_tiles)

    share = CG * tile // 2
    keep, send = pl.pallas_call(
        back_kernel,
        out_shape=(jax.ShapeDtypeStruct((share, 3 * CG * tile), jnp.bfloat16),) * 2,
        in_specs=[vmem] * 4,
        out_specs=(vmem, vmem),
        scratch_shapes=[pltpu.VMEM((2, HALO * tile, CG * tile), jnp.bfloat16)],
        compiler_params=pltpu.CompilerParams(vmem_limit_bytes=24 * 2**20),
        cost_estimate=pl.CostEstimate(flops=3 * 10**8, bytes_accessed=3 * 2**20, transcendentals=0),
        name="back",
    )(g, own, *halos)
    other = lax.ppermute(send, "sub", [(i, i ^ 1) for i in range(members)])
    chip = (keep.astype(jnp.float32) + other.astype(jnp.float32)).astype(jnp.bfloat16)
    parts = chip.reshape(members // 2, -1, chip.shape[1])
    total = parts[0].astype(jnp.float32)
    for turn in range(1, members // 2):
        route = [(i, i ^ (2 * TURNS[i % 2][turn - 1])) for i in range(members)]
        total += lax.ppermute(parts[turn], "sub", route).astype(jnp.float32)
    return total


def solution(mesh):
    in_specs = (
        P(("dom", "sub"), None, None, None),
        P(("dom", "sub"), None),
        P(("dom", "sub")),
        P(("dom", "sub")),
        P(("dom", "sub"), None, None),
    )
    out_specs = P(("dom", "sub"), None)
    body = functools.partial(local, mesh.shape["dom"], mesh.shape["sub"])
    return jax.shard_map(body, mesh=mesh, in_specs=in_specs, out_specs=out_specs, check_vma=False)
```

```python
import functools

import jax
import jax.numpy as jnp
from jax import lax
from jax.experimental import pallas as pl
from jax.experimental.pallas import tpu as pltpu
from jax.sharding import PartitionSpec as P

CG = 4
HALO = 2
TURNS = ((2, 1, 3), (3, 1, 2))
MARK = 16


def pack_kernel(agg_hbm, p_hbm, first_ref, second_ref, agg_ref, ends_ref, sems):
    rows, tile = p_hbm.shape[0], p_hbm.shape[1]
    copies = [
        pltpu.make_async_copy(agg_hbm, agg_ref, sems.at[0]),
        pltpu.make_async_copy(p_hbm.at[pl.ds(0, HALO)], ends_ref.at[0], sems.at[1]),
        pltpu.make_async_copy(p_hbm.at[pl.ds(rows - HALO, HALO)], ends_ref.at[1], sems.at[2]),
    ]
    for copy in copies:
        copy.start()
    for copy in copies:
        copy.wait()
    odd = lax.rem(agg_ref[0] // CG, 2)
    for turn, ref in enumerate((first_ref, second_ref)):
        tail = 1 - odd if turn == 0 else odd
        for r in range(HALO):
            mark = lax.rem(agg_ref[tail * (rows - HALO) + r], CG) + (1 - tail) * CG
            ref[r, pl.ds(0, tile), :] = ends_ref[tail, r]
            ref[r, pl.ds(tile, MARK), :] = jnp.full((MARK, tile), mark.astype(jnp.float32)).astype(jnp.bfloat16)


def turn_of(apart, core):
    place = 0
    for turn, step in enumerate(TURNS[core], start=1):
        place = jnp.where(apart == step, turn, place)
    return place


def front_kernel(
    groups, members, col_ref, count_ref, agg_ref, a_ref, p_ref,
    g_ref, gown_ref, place_ref, acc_ref, pt_ref,
):
    rows, slots, tile = a_ref.shape[0], a_ref.shape[1], a_ref.shape[2]
    columns = rows + 2 * HALO
    half = tile // 2
    acc_ref[...] = jnp.zeros_like(acc_ref)
    device = col_ref[0, 0] // rows
    my_group = device // members
    core = lax.rem(device, 2)
    chip = lax.rem(device, members) // 2
    for r in range(rows):
        coarse = lax.rem(agg_ref[r], CG)
        p_r = p_ref[r]
        pt_ref[r] = p_r.T
        for j in range(CG):
            place_ref[pl.ds(r * tile, tile), pl.ds(j * tile, tile)] = jnp.where(coarse == j, p_r, jnp.zeros_like(p_r))
    for t in range(rows):
        for pair in range(slots // 2):
            both = jnp.concatenate([a_ref[t, 2 * pair], a_ref[t, 2 * pair + 1]], axis=1)
            terms = jnp.dot(pt_ref[t], both, preferred_element_type=jnp.float32)
            for side in range(2):
                k = 2 * pair + side
                column = col_ref[t, k]
                offset = lax.rem(column // (rows * members) - my_group + 1 + groups, groups)
                near = lax.rem(column, rows) + rows * offset - (rows - HALO)
                at = jnp.where(k < count_ref[t], lax.rem(agg_ref[t], CG) * columns + near, CG * columns)
                at = jnp.clip(at, 0, CG * columns)
                acc_ref[at] += terms[:, side * tile : (side + 1) * tile]
    for i in range(CG):
        for part in range(2):
            first = pl.multiple_of((core if part == 1 else 1 - core) * half, half)
            turn = jnp.where(core == 1 - part, turn_of(i ^ chip, 0), turn_of(i ^ chip, 1))
            to = pl.ds(pl.multiple_of((part * CG + turn) * half, half), half)
            for c in range(columns):
                block = acc_ref[i * columns + c, pl.ds(first, half), :].astype(jnp.bfloat16)
                if c < HALO:
                    g_ref[to, pl.ds(c * tile, tile)] = block
                elif c >= HALO + rows:
                    g_ref[to, pl.ds((c - rows) * tile, tile)] = block
                else:
                    gown_ref[to, pl.ds((c - HALO) * tile, tile)] = block


def back_kernel(half, g_ref, gown_ref, placed_ref, first_ref, second_ref, out_ref, place_ref):
    tile = first_ref.shape[2]
    rows = out_ref.shape[0]
    for r in range(HALO):
        tiles = [ref[r, pl.ds(0, tile), :] for ref in (first_ref, second_ref)]
        marks = [ref[r, pl.ds(tile, MARK), :].astype(jnp.float32)[0:1, :] for ref in (first_ref, second_ref)]
        for side in range(2):
            for j in range(CG):
                chosen = [jnp.where(mark == float(side * CG + j), 1.0, 0.0).astype(jnp.bfloat16) for mark in marks]
                place_ref[side, pl.ds(r * tile, tile), pl.ds(j * tile, tile)] = tiles[0] * chosen[0] + tiles[1] * chosen[1]
    width = CG * tile
    depth = HALO * tile
    at = pl.ds(half * rows, rows)
    own = jnp.dot(gown_ref[at, :], placed_ref[...], preferred_element_type=jnp.float32)
    out_ref[:, pl.ds(width, width)] = own.astype(jnp.bfloat16)
    for side in range(2):
        columns = g_ref[at, pl.ds(side * depth, depth)]
        result = jnp.dot(columns, place_ref[side], preferred_element_type=jnp.float32)
        out_ref[:, pl.ds(2 * side * width, width)] = result.astype(jnp.bfloat16)


def local(groups, members, a_tiles, col_tiles, counts, aggregate, p_tiles):
    rows, slots, tile = a_tiles.shape[0], a_tiles.shape[1], a_tiles.shape[2]
    columns = rows + 2 * HALO
    hbm = pl.BlockSpec(memory_space=pltpu.HBM)
    smem = pl.BlockSpec(memory_space=pltpu.SMEM)
    keep_in_hbm = functools.partial(pltpu.with_memory_space_constraint, memory_space=pltpu.HBM)
    vmem = pl.BlockSpec(memory_space=pltpu.VMEM)
    blocks = pl.pallas_call(
        pack_kernel,
        out_shape=(jax.ShapeDtypeStruct((HALO, tile + MARK, tile), jnp.bfloat16),) * 2,
        in_specs=[hbm, hbm],
        out_specs=(vmem, vmem),
        scratch_shapes=[
            pltpu.SMEM(aggregate.shape, jnp.int32),
            pltpu.VMEM((2, HALO, tile, tile), jnp.bfloat16),
            pltpu.SemaphoreType.DMA((3,)),
        ],
        cost_estimate=pl.CostEstimate(flops=10**9, bytes_accessed=64 * 2**20, transcendentals=0),
        name="pack",
    )(keep_in_hbm(aggregate), keep_in_hbm(p_tiles))
    halos = []
    for turn, block in enumerate(blocks):
        route = []
        for i in range(turn, groups + turn, 2):
            route += [(i % groups, (i + 1) % groups), ((i + 1) % groups, i % groups)]
        halos.append(lax.ppermute(block, "dom", route))

    operands = pl.pallas_call(
        functools.partial(front_kernel, groups, members),
        out_shape=(
            jax.ShapeDtypeStruct((CG * tile, 2 * HALO * tile), jnp.bfloat16),
            jax.ShapeDtypeStruct((CG * tile, rows * tile), jnp.bfloat16),
            jax.ShapeDtypeStruct((rows * tile, CG * tile), jnp.bfloat16),
        ),
        in_specs=[smem] * 3 + [vmem] * 2,
        out_specs=(vmem,) * 3,
        scratch_shapes=[
            pltpu.VMEM((CG * columns + 1, tile, tile), jnp.float32),
            pltpu.VMEM(p_tiles.shape, jnp.bfloat16),
        ],
        compiler_params=pltpu.CompilerParams(vmem_limit_bytes=24 * 2**20),
        cost_estimate=pl.CostEstimate(flops=2 * 10**9, bytes_accessed=4 * 2**20, transcendentals=0),
        name="front",
    )(col_tiles, counts, aggregate, a_tiles, p_tiles)

    def rows_of(half):
        return pl.pallas_call(
            functools.partial(back_kernel, half),
            out_shape=jax.ShapeDtypeStruct((CG * tile // 2, 3 * CG * tile), jnp.bfloat16),
            in_specs=[vmem] * 5,
            out_specs=vmem,
            scratch_shapes=[pltpu.VMEM((2, HALO * tile, CG * tile), jnp.bfloat16)],
            compiler_params=pltpu.CompilerParams(vmem_limit_bytes=24 * 2**20),
            cost_estimate=pl.CostEstimate(flops=4 * 10**8, bytes_accessed=4 * 2**20, transcendentals=0),
            name="back",
        )(*operands, *halos)

    other = lax.ppermute(rows_of(0), "sub", [(i, i ^ 1) for i in range(members)])
    keep = rows_of(1)
    chip = (keep.astype(jnp.float32) + other.astype(jnp.float32)).astype(jnp.bfloat16)
    parts = chip.reshape(members // 2, -1, chip.shape[1])
    total = parts[0].astype(jnp.float32)
    for turn in range(1, members // 2):
        route = [(i, i ^ (2 * TURNS[i % 2][turn - 1])) for i in range(members)]
        total += lax.ppermute(parts[turn], "sub", route).astype(jnp.float32)
    return total


def solution(mesh):
    in_specs = (
        P(("dom", "sub"), None, None, None),
        P(("dom", "sub"), None),
        P(("dom", "sub")),
        P(("dom", "sub")),
        P(("dom", "sub"), None, None),
    )
    out_specs = P(("dom", "sub"), None)
    body = functools.partial(local, mesh.shape["dom"], mesh.shape["sub"])
    return jax.shard_map(body, mesh=mesh, in_specs=in_specs, out_specs=out_specs, check_vma=False)
```

```python
import functools

import jax
import jax.numpy as jnp
from jax import lax
from jax.experimental import pallas as pl
from jax.experimental.pallas import tpu as pltpu
from jax.sharding import PartitionSpec as P

CG = 4
HALO = 2
TURNS = ((2, 1, 3), (3, 1, 2))
MARK = 16


def pack_kernel(agg_hbm, p_hbm, first_ref, second_ref, agg_ref, ends_ref, sems):
    rows, tile = p_hbm.shape[0], p_hbm.shape[1]
    copies = [
        pltpu.make_async_copy(agg_hbm, agg_ref, sems.at[0]),
        pltpu.make_async_copy(p_hbm.at[pl.ds(0, HALO)], ends_ref.at[0], sems.at[1]),
        pltpu.make_async_copy(p_hbm.at[pl.ds(rows - HALO, HALO)], ends_ref.at[1], sems.at[2]),
    ]
    for copy in copies:
        copy.start()
    for copy in copies:
        copy.wait()
    odd = lax.rem(agg_ref[0] // CG, 2)
    for turn, ref in enumerate((first_ref, second_ref)):
        tail = 1 - odd if turn == 0 else odd
        for r in range(HALO):
            mark = lax.rem(agg_ref[tail * (rows - HALO) + r], CG) + (1 - tail) * CG
            ref[r, pl.ds(0, tile), :] = ends_ref[tail, r]
            ref[r, pl.ds(tile, MARK), :] = jnp.full((MARK, tile), mark.astype(jnp.float32)).astype(jnp.bfloat16)


def turn_of(apart, core):
    place = 0
    for turn, step in enumerate(TURNS[core], start=1):
        place = jnp.where(apart == step, turn, place)
    return place


def front_kernel(
    groups, members, col_ref, count_ref, agg_ref, a_ref, p_ref,
    g_ref, gown_ref, place_ref, acc_ref, pt_ref,
):
    rows, slots, tile = a_ref.shape[0], a_ref.shape[1], a_ref.shape[2]
    columns = rows + 2 * HALO
    half = tile // 2
    acc_ref[...] = jnp.zeros_like(acc_ref)
    device = col_ref[0, 0] // rows
    my_group = device // members
    core = lax.rem(device, 2)
    chip = lax.rem(device, members) // 2
    for r in range(rows):
        coarse = lax.rem(agg_ref[r], CG)
        p_r = p_ref[r]
        pt_ref[r] = p_r.T
        for j in range(CG):
            place_ref[pl.ds(r * tile, tile), pl.ds(j * tile, tile)] = jnp.where(coarse == j, p_r, jnp.zeros_like(p_r))
    for t in range(rows):
        for pair in range(slots // 2):
            both = jnp.concatenate([a_ref[t, 2 * pair], a_ref[t, 2 * pair + 1]], axis=1)
            terms = jnp.dot(pt_ref[t], both, preferred_element_type=jnp.float32)
            for side in range(2):
                k = 2 * pair + side
                column = col_ref[t, k]
                offset = lax.rem(column // (rows * members) - my_group + 1 + groups, groups)
                near = lax.rem(column, rows) + rows * offset - (rows - HALO)
                at = jnp.where(k < count_ref[t], lax.rem(agg_ref[t], CG) * columns + near, CG * columns)
                at = jnp.clip(at, 0, CG * columns)
                acc_ref[at] += terms[:, side * tile : (side + 1) * tile]
    for i in range(CG):
        for part in range(2):
            first = pl.multiple_of((core if part == 1 else 1 - core) * half, half)
            turn = jnp.where(core == 1 - part, turn_of(i ^ chip, 0), turn_of(i ^ chip, 1))
            to = pl.ds(pl.multiple_of((part * CG + turn) * half, half), half)
            for c in range(columns):
                block = acc_ref[i * columns + c, pl.ds(first, half), :].astype(jnp.bfloat16)
                if c < HALO:
                    g_ref[to, pl.ds(c * tile, tile)] = block
                elif c >= HALO + rows:
                    g_ref[to, pl.ds((c - rows) * tile, tile)] = block
                else:
                    gown_ref[to, pl.ds((c - HALO) * tile, tile)] = block


def back_kernel(half, g_ref, gown_ref, placed_ref, first_ref, second_ref, out_ref, place_ref):
    tile = first_ref.shape[2]
    rows = out_ref.shape[0]
    for r in range(HALO):
        tiles = [ref[r, pl.ds(0, tile), :] for ref in (first_ref, second_ref)]
        marks = [ref[r, pl.ds(tile, MARK), :].astype(jnp.float32)[0:1, :] for ref in (first_ref, second_ref)]
        for side in range(2):
            for j in range(CG):
                chosen = [jnp.where(mark == float(side * CG + j), 1.0, 0.0).astype(jnp.bfloat16) for mark in marks]
                place_ref[side, pl.ds(r * tile, tile), pl.ds(j * tile, tile)] = tiles[0] * chosen[0] + tiles[1] * chosen[1]
    width = CG * tile
    depth = HALO * tile
    at = pl.ds(half * rows, rows)
    own = jnp.dot(gown_ref[at, :], placed_ref[...], preferred_element_type=jnp.float32)
    out_ref[:, pl.ds(width, width)] = own.astype(jnp.bfloat16)
    for side in range(2):
        columns = g_ref[at, pl.ds(side * depth, depth)]
        result = jnp.dot(columns, place_ref[side], preferred_element_type=jnp.float32)
        out_ref[:, pl.ds(2 * side * width, width)] = result.astype(jnp.bfloat16)


def local(groups, members, a_tiles, col_tiles, counts, aggregate, p_tiles):
    rows, slots, tile = a_tiles.shape[0], a_tiles.shape[1], a_tiles.shape[2]
    columns = rows + 2 * HALO
    hbm = pl.BlockSpec(memory_space=pltpu.HBM)
    smem = pl.BlockSpec(memory_space=pltpu.SMEM)
    keep_in_hbm = functools.partial(pltpu.with_memory_space_constraint, memory_space=pltpu.HBM)
    vmem = pl.BlockSpec(memory_space=pltpu.VMEM)
    blocks = pl.pallas_call(
        pack_kernel,
        out_shape=(jax.ShapeDtypeStruct((HALO, tile + MARK, tile), jnp.bfloat16),) * 2,
        in_specs=[hbm, hbm],
        out_specs=(vmem, vmem),
        scratch_shapes=[
            pltpu.SMEM(aggregate.shape, jnp.int32),
            pltpu.VMEM((2, HALO, tile, tile), jnp.bfloat16),
            pltpu.SemaphoreType.DMA((3,)),
        ],
        cost_estimate=pl.CostEstimate(flops=10**9, bytes_accessed=64 * 2**20, transcendentals=0),
        name="pack",
    )(keep_in_hbm(aggregate), keep_in_hbm(p_tiles))
    halos = []
    for turn, block in enumerate(blocks):
        route = []
        for i in range(turn, groups + turn, 2):
            route += [(i % groups, (i + 1) % groups), ((i + 1) % groups, i % groups)]
        halos.append(lax.ppermute(block, "dom", route))

    operands = pl.pallas_call(
        functools.partial(front_kernel, groups, members),
        out_shape=(
            jax.ShapeDtypeStruct((CG * tile, 2 * HALO * tile), jnp.bfloat16),
            jax.ShapeDtypeStruct((CG * tile, rows * tile), jnp.bfloat16),
            jax.ShapeDtypeStruct((rows * tile, CG * tile), jnp.bfloat16),
        ),
        in_specs=[smem] * 3 + [vmem] * 2,
        out_specs=(vmem,) * 3,
        scratch_shapes=[
            pltpu.VMEM((CG * columns + 1, tile, tile), jnp.float32),
            pltpu.VMEM(p_tiles.shape, jnp.bfloat16),
        ],
        compiler_params=pltpu.CompilerParams(vmem_limit_bytes=24 * 2**20),
        cost_estimate=pl.CostEstimate(flops=2 * 10**9, bytes_accessed=4 * 2**20, transcendentals=0),
        name="front",
    )(col_tiles, counts, aggregate, a_tiles, p_tiles)

    def rows_of(half):
        return pl.pallas_call(
            functools.partial(back_kernel, half),
            out_shape=jax.ShapeDtypeStruct((CG * tile // 2, 3 * CG * tile), jnp.bfloat16),
            in_specs=[vmem] * 5,
            out_specs=vmem,
            scratch_shapes=[pltpu.VMEM((2, HALO * tile, CG * tile), jnp.bfloat16)],
            compiler_params=pltpu.CompilerParams(vmem_limit_bytes=24 * 2**20),
            cost_estimate=pl.CostEstimate(flops=4 * 10**8, bytes_accessed=4 * 2**20, transcendentals=0),
            name="back",
        )(*operands, *halos)

    other = lax.ppermute(rows_of(0), "sub", [(i, i ^ 1) for i in range(members)])
    keep = rows_of(1)
    share = keep.shape[0] // (members // 2)
    parts = []
    for turn in range(members // 2):
        at = slice(turn * share, (turn + 1) * share)
        parts.append(keep[at].astype(jnp.float32) + other[at].astype(jnp.float32))
    total = parts[0]
    for turn in range(1, members // 2):
        route = [(i, i ^ (2 * TURNS[i % 2][turn - 1])) for i in range(members)]
        total += lax.ppermute(parts[turn].astype(jnp.bfloat16), "sub", route).astype(jnp.float32)
    return total


def solution(mesh):
    in_specs = (
        P(("dom", "sub"), None, None, None),
        P(("dom", "sub"), None),
        P(("dom", "sub")),
        P(("dom", "sub")),
        P(("dom", "sub"), None, None),
    )
    out_specs = P(("dom", "sub"), None)
    body = functools.partial(local, mesh.shape["dom"], mesh.shape["sub"])
    return jax.shard_map(body, mesh=mesh, in_specs=in_specs, out_specs=out_specs, check_vma=False)
```

```python
import functools

import jax
import jax.numpy as jnp
from jax import lax
from jax.experimental import pallas as pl
from jax.experimental.pallas import tpu as pltpu
from jax.sharding import PartitionSpec as P

CG = 4
HALO = 2
TURNS = ((2, 3, 1), (2, 1, 3))
MARK = 16


def pack_kernel(agg_hbm, p_hbm, first_ref, second_ref, agg_ref, ends_ref, sems):
    rows, tile = p_hbm.shape[0], p_hbm.shape[1]
    copies = [
        pltpu.make_async_copy(agg_hbm, agg_ref, sems.at[0]),
        pltpu.make_async_copy(p_hbm.at[pl.ds(0, HALO)], ends_ref.at[0], sems.at[1]),
        pltpu.make_async_copy(p_hbm.at[pl.ds(rows - HALO, HALO)], ends_ref.at[1], sems.at[2]),
    ]
    for copy in copies:
        copy.start()
    for copy in copies:
        copy.wait()
    odd = lax.rem(agg_ref[0] // CG, 2)
    for turn, ref in enumerate((first_ref, second_ref)):
        tail = 1 - odd if turn == 0 else odd
        for r in range(HALO):
            mark = lax.rem(agg_ref[tail * (rows - HALO) + r], CG) + (1 - tail) * CG
            ref[r, pl.ds(0, tile), :] = ends_ref[tail, r]
            ref[r, pl.ds(tile, MARK), :] = jnp.full((MARK, tile), mark.astype(jnp.float32)).astype(jnp.bfloat16)


def turn_of(apart, core):
    place = 0
    for turn, step in enumerate(TURNS[core], start=1):
        place = jnp.where(apart == step, turn, place)
    return place


def front_kernel(
    groups, members, col_ref, count_ref, agg_ref, a_ref, p_ref,
    g_ref, gown_ref, place_ref, acc_ref, pt_ref,
):
    rows, slots, tile = a_ref.shape[0], a_ref.shape[1], a_ref.shape[2]
    columns = rows + 2 * HALO
    half = tile // 2
    acc_ref[...] = jnp.zeros_like(acc_ref)
    device = col_ref[0, 0] // rows
    my_group = device // members
    core = lax.rem(device, 2)
    chip = lax.rem(device, members) // 2
    for r in range(rows):
        coarse = lax.rem(agg_ref[r], CG)
        p_r = p_ref[r]
        pt_ref[r] = p_r.T
        for j in range(CG):
            place_ref[pl.ds(r * tile, tile), pl.ds(j * tile, tile)] = jnp.where(coarse == j, p_r, jnp.zeros_like(p_r))
    for t in range(rows):
        for pair in range(slots // 2):
            both = jnp.concatenate([a_ref[t, 2 * pair], a_ref[t, 2 * pair + 1]], axis=1)
            terms = jnp.dot(pt_ref[t], both, preferred_element_type=jnp.float32)
            for side in range(2):
                k = 2 * pair + side
                column = col_ref[t, k]
                offset = lax.rem(column // (rows * members) - my_group + 1 + groups, groups)
                near = lax.rem(column, rows) + rows * offset - (rows - HALO)
                at = jnp.where(k < count_ref[t], lax.rem(agg_ref[t], CG) * columns + near, CG * columns)
                at = jnp.clip(at, 0, CG * columns)
                acc_ref[at] += terms[:, side * tile : (side + 1) * tile]
    for i in range(CG):
        for part in range(2):
            first = pl.multiple_of((core if part == 1 else 1 - core) * half, half)
            turn = jnp.where(core == 1 - part, turn_of(i ^ chip, 0), turn_of(i ^ chip, 1))
            to = pl.ds(pl.multiple_of((part * CG + turn) * half, half), half)
            for c in range(columns):
                block = acc_ref[i * columns + c, pl.ds(first, half), :].astype(jnp.bfloat16)
                if c < HALO:
                    g_ref[to, pl.ds(c * tile, tile)] = block
                elif c >= HALO + rows:
                    g_ref[to, pl.ds((c - rows) * tile, tile)] = block
                else:
                    gown_ref[to, pl.ds((c - HALO) * tile, tile)] = block


def back_kernel(half, g_ref, gown_ref, placed_ref, first_ref, second_ref, out_ref, place_ref):
    tile = first_ref.shape[2]
    rows = out_ref.shape[0]
    for r in range(HALO):
        tiles = [ref[r, pl.ds(0, tile), :] for ref in (first_ref, second_ref)]
        marks = [ref[r, pl.ds(tile, MARK), :].astype(jnp.float32)[0:1, :] for ref in (first_ref, second_ref)]
        for side in range(2):
            for j in range(CG):
                chosen = [jnp.where(mark == float(side * CG + j), 1.0, 0.0).astype(jnp.bfloat16) for mark in marks]
                place_ref[side, pl.ds(r * tile, tile), pl.ds(j * tile, tile)] = tiles[0] * chosen[0] + tiles[1] * chosen[1]
    width = CG * tile
    depth = HALO * tile
    at = pl.ds(half * rows, rows)
    own = jnp.dot(gown_ref[at, :], placed_ref[...], preferred_element_type=jnp.float32)
    out_ref[:, pl.ds(width, width)] = own.astype(jnp.bfloat16)
    for side in range(2):
        columns = g_ref[at, pl.ds(side * depth, depth)]
        result = jnp.dot(columns, place_ref[side], preferred_element_type=jnp.float32)
        out_ref[:, pl.ds(2 * side * width, width)] = result.astype(jnp.bfloat16)


def local(groups, members, a_tiles, col_tiles, counts, aggregate, p_tiles):
    rows, slots, tile = a_tiles.shape[0], a_tiles.shape[1], a_tiles.shape[2]
    columns = rows + 2 * HALO
    hbm = pl.BlockSpec(memory_space=pltpu.HBM)
    smem = pl.BlockSpec(memory_space=pltpu.SMEM)
    keep_in_hbm = functools.partial(pltpu.with_memory_space_constraint, memory_space=pltpu.HBM)
    vmem = pl.BlockSpec(memory_space=pltpu.VMEM)
    blocks = pl.pallas_call(
        pack_kernel,
        out_shape=(jax.ShapeDtypeStruct((HALO, tile + MARK, tile), jnp.bfloat16),) * 2,
        in_specs=[hbm, hbm],
        out_specs=(vmem, vmem),
        scratch_shapes=[
            pltpu.SMEM(aggregate.shape, jnp.int32),
            pltpu.VMEM((2, HALO, tile, tile), jnp.bfloat16),
            pltpu.SemaphoreType.DMA((3,)),
        ],
        cost_estimate=pl.CostEstimate(flops=10**9, bytes_accessed=64 * 2**20, transcendentals=0),
        name="pack",
    )(keep_in_hbm(aggregate), keep_in_hbm(p_tiles))
    halos = []
    for turn, block in enumerate(blocks):
        route = []
        for i in range(turn, groups + turn, 2):
            route += [(i % groups, (i + 1) % groups), ((i + 1) % groups, i % groups)]
        halos.append(lax.ppermute(block, "dom", route))

    operands = pl.pallas_call(
        functools.partial(front_kernel, groups, members),
        out_shape=(
            jax.ShapeDtypeStruct((CG * tile, 2 * HALO * tile), jnp.bfloat16),
            jax.ShapeDtypeStruct((CG * tile, rows * tile), jnp.bfloat16),
            jax.ShapeDtypeStruct((rows * tile, CG * tile), jnp.bfloat16),
        ),
        in_specs=[smem] * 3 + [vmem] * 2,
        out_specs=(vmem,) * 3,
        scratch_shapes=[
            pltpu.VMEM((CG * columns + 1, tile, tile), jnp.float32),
            pltpu.VMEM(p_tiles.shape, jnp.bfloat16),
        ],
        compiler_params=pltpu.CompilerParams(vmem_limit_bytes=24 * 2**20),
        cost_estimate=pl.CostEstimate(flops=2 * 10**9, bytes_accessed=4 * 2**20, transcendentals=0),
        name="front",
    )(col_tiles, counts, aggregate, a_tiles, p_tiles)

    def rows_of(half):
        return pl.pallas_call(
            functools.partial(back_kernel, half),
            out_shape=jax.ShapeDtypeStruct((CG * tile // 2, 3 * CG * tile), jnp.bfloat16),
            in_specs=[vmem] * 5,
            out_specs=vmem,
            scratch_shapes=[pltpu.VMEM((2, HALO * tile, CG * tile), jnp.bfloat16)],
            compiler_params=pltpu.CompilerParams(vmem_limit_bytes=24 * 2**20),
            cost_estimate=pl.CostEstimate(flops=4 * 10**8, bytes_accessed=4 * 2**20, transcendentals=0),
            name="back",
        )(*operands, *halos)

    other = lax.ppermute(rows_of(0), "sub", [(i, i ^ 1) for i in range(members)])
    keep = rows_of(1)
    chip = (keep.astype(jnp.float32) + other.astype(jnp.float32)).astype(jnp.bfloat16)
    parts = chip.reshape(members // 2, -1, chip.shape[1])
    total = parts[0].astype(jnp.float32)
    for turn in range(1, members // 2):
        route = [(i, i ^ (2 * TURNS[i % 2][turn - 1])) for i in range(members)]
        total += lax.ppermute(parts[turn], "sub", route).astype(jnp.float32)
    return total


def solution(mesh):
    in_specs = (
        P(("dom", "sub"), None, None, None),
        P(("dom", "sub"), None),
        P(("dom", "sub")),
        P(("dom", "sub")),
        P(("dom", "sub"), None, None),
    )
    out_specs = P(("dom", "sub"), None)
    body = functools.partial(local, mesh.shape["dom"], mesh.shape["sub"])
    return jax.shard_map(body, mesh=mesh, in_specs=in_specs, out_specs=out_specs, check_vma=False)
```
